32 devices in a mesh: grp: 2 (over y), hot: 4 (over x, core), patch: 4 (over z).
Axes of the slice: x: 2, y: 2, z: 4, core: 2. Of those that a mesh axis runs over, the one named last changes fastest.
Arguments:
- influence: bfloat16 [3, 4096, 4096], P(None, 'hot', 'patch'), may hold values from -0.09375 to 0.09375
- loads: bfloat16 [8192, 128], P('grp'), parts along dimension 0, may hold values from -6 to 6
- patch_order: int32 [4096], replicated, may hold values from 0 to 4095, each once
- spectral_weights: float32 [128], P('grp'), parts along dimension 0, may hold values from 0.005 to 0.05
- block_position: int32 [4096], replicated, may hold values from 0 to 4095, as said below
- block_pairs: int32 [48, 2], P(('hot', 'patch')), may hold values from 0 to 15, as said below
Outputs:
- cross_spectra: bfloat16 [96, 2, 768, 768], P(('grp', 'hot', 'patch')), parts along dimension 0
The draws below stay inside these ranges and needn't reach their ends.
There are 2 independent parts, one for each index of `grp`. The reference program is written for one: setup_inputs(seed, part) draws one part's arguments, and reference() takes and returns one part's arrays. A program takes and returns all parts, laid end to end along the dimension named above; an argument that names none is the same for every part. Nothing has to cross between parts.
Inputs may be any that keep to these rules, and one draw needn't show every extreme that they name: `patch_order`: a permutation of the patches. `block_position`: a permutation of the hotspots; hotspots h * 1024 to (h + 1) * 1024 - 1 send exactly 256 of their rows into every range of rows d * 1024 to (d + 1) * 1024 - 1 of block order. `block_pairs`: each row holds two block numbers, the first not greater than the second; pairs may repeat.
All inputs are finite; a program needn't handle non-finite values.
Results may differ from the reference program's by a relative error of at most 0.0064.
Values may be sent and summed in bfloat16 or wider, within the bound.
No kernel may reach another device: no remote copies, remote signals or barrier semaphores. Data moves between devices by JAX's collectives and lax.ppermute only.
A program may use at most 128 MiB of HBM per device.

```python
import math
import jax
import jax.numpy as jnp
from jax import lax

NC = 3
CASES = 64
BLK = 256
PATCHES = 4096
HOT_DEV = 1024
SHARE = 256
HOTSPOTS = 4096
BLOCKS = 16
PAIRS = 48
N_HOT = 4


def draw_block_position(key, part):
    first_key, second_key = jax.random.split(jax.random.fold_in(key, 11), 2)
    source_keys = jax.random.split(first_key, N_HOT)
    owner_keys = jax.random.split(second_key, N_HOT)
    local_rank = jax.vmap(lambda one_key: jax.random.permutation(one_key, HOT_DEV))(source_keys).astype(jnp.int32)
    slot_order = jax.vmap(lambda one_key: jax.random.permutation(one_key, HOT_DEV))(owner_keys).astype(jnp.int32)
    owner_index = local_rank // SHARE
    source_index = jnp.arange(N_HOT, dtype=jnp.int32)[:, None]
    incoming_slot = source_index * SHARE + local_rank % SHARE
    position = owner_index * HOT_DEV + slot_order[owner_index, incoming_slot]
    return position.reshape(-1).astype(jnp.int32)


def draw_block_pairs(key, part):
    first_key, second_key = jax.random.split(jax.random.fold_in(key, 23), 2)
    first_block = jax.random.randint(first_key, (PAIRS,), 0, BLOCKS, dtype=jnp.int32)
    second_block = jax.random.randint(second_key, (PAIRS,), 0, BLOCKS, dtype=jnp.int32)
    lower_block = jnp.minimum(first_block, second_block)
    upper_block = jnp.maximum(first_block, second_block)
    return jnp.stack([lower_block, upper_block], axis=1).astype(jnp.int32)


def levels(rng, dims, pieces, low, top_value):
    gain = 1.0
    for axis_at, parts in pieces:
        steps = jax.random.uniform(jax.random.fold_in(jax.random.fold_in(rng, 6), axis_at), (parts,), jnp.float32, low / len(pieces), top_value / len(pieces))
        gain = gain * jnp.repeat(jnp.exp(steps), dims[axis_at] // parts).reshape((-1,) + (1,) * (len(dims) - 1 - axis_at))
    return gain


def gaussian(own_key, shape, scale, most, pieces=(), kind=jnp.bfloat16):
    level = levels(own_key, shape, pieces, -0.22, 0.18) if pieces else 1.0
    entries = jax.random.normal(own_key, shape, jnp.float32) * scale * level
    return jnp.minimum(jnp.maximum(entries, -most), most).astype(kind)


def setup_inputs(seed: int = 0, part: int = 0) -> dict:
    seeds = jax.random.split(jax.random.key(seed), 7)
    own_keys = jax.random.split(jax.random.fold_in(seeds[6], part), 7)
    return {
        "influence": gaussian(seeds[0], (NC, HOTSPOTS, PATCHES), PATCHES ** -0.5, 0.09375, ((1, 4), (2, 4))),
        "loads": gaussian(own_keys[1], (PATCHES, 2 * CASES), 1.0, 6.0),
        "patch_order": jax.random.permutation(seeds[2], PATCHES).astype(jnp.int32),
        "spectral_weights": jnp.clip(jnp.exp(jax.random.uniform(own_keys[3], (CASES,), jnp.float32, math.log(0.005), math.log(0.05))), 0.005, 0.05),
        "block_position": draw_block_position(jax.random.fold_in(seeds[6], 71), part),
        "block_pairs": draw_block_pairs(jax.random.fold_in(seeds[6], 71), part),
    }


def reference(influence, loads, patch_order, spectral_weights, block_position, block_pairs):
    components = influence.shape[0]
    hotspots = influence.shape[1]
    columns = loads.shape[1]
    half_cols = columns // 2
    loads_by_column = jnp.take(loads, patch_order, axis=0)
    flat_influence = influence.reshape(components * hotspots, influence.shape[2])
    stress_full = jnp.dot(flat_influence, loads_by_column, preferred_element_type=jnp.float32)
    stress = jnp.transpose(stress_full.reshape(components, hotspots, columns), (1, 0, 2))
    stress = stress.reshape(hotspots, components * columns).astype(jnp.bfloat16)
    inverse = jnp.zeros((hotspots,), jnp.int32).at[block_position].set(jnp.arange(hotspots, dtype=jnp.int32))
    blocked = jnp.take(stress, inverse, axis=0)
    weights_row = jnp.concatenate([spectral_weights, spectral_weights]).astype(jnp.float32)
    contract_dims = (((1,), (1,)), ((), ()))

    def one_pair(pair_ids):
        left_rows = lax.dynamic_slice_in_dim(blocked, pair_ids[0] * BLK, BLK, 0).reshape(BLK * components, columns)
        right_rows = lax.dynamic_slice_in_dim(blocked, pair_ids[1] * BLK, BLK, 0).reshape(BLK * components, columns)
        scaled = (left_rows.astype(jnp.float32) * weights_row).astype(jnp.bfloat16)
        rotated = jnp.concatenate([-right_rows[:, half_cols:], right_rows[:, :half_cols]], axis=1)
        real_part = lax.dot_general(scaled, right_rows, contract_dims, preferred_element_type=jnp.float32)
        imag_part = lax.dot_general(scaled, rotated, contract_dims, preferred_element_type=jnp.float32)
        return jnp.stack([real_part, imag_part]).astype(jnp.bfloat16)

    return lax.map(one_pair, block_pairs)
```

```python
import functools

import jax
import jax.numpy as jnp
from jax import lax
from jax.experimental import pallas as pl
from jax.experimental.pallas import tpu as pltpu
from jax.sharding import PartitionSpec as P

BLK = 256
LANES = 128
F32 = jnp.float32
BF16 = jnp.bfloat16
VMEM_BYTES = 48 * 1024 * 1024


def params(steps=1):
    return pltpu.CompilerParams(
        dimension_semantics=("arbitrary",) * steps, vmem_limit_bytes=VMEM_BYTES
    )


def share_product(influence_ref, my_loads, out_ref):
    columns = my_loads.shape[1]
    for c in range(influence_ref.shape[0]):
        part = jnp.dot(influence_ref[c], my_loads, preferred_element_type=F32)
        out_ref[:, c * columns : (c + 1) * columns] = part.astype(out_ref.dtype)


def gather_kernel(index_ref, order_ref, loads_ref, *refs):
    shares = (len(refs) - 2) // 2
    influence_refs, out_refs = refs[:shares], refs[shares : 2 * shares]
    my_loads_ref, pick_ref = refs[2 * shares :]
    patches = loads_ref.shape[0]
    lane = lax.broadcasted_iota(jnp.int32, (LANES, LANES), 1)
    for g in range(order_ref.shape[1]):
        row = jnp.broadcast_to(order_ref[0, g : g + 1, :], (LANES, LANES))
        wanted = jnp.transpose(row) - lane
        for j in range(patches // LANES):
            pick_ref[g * LANES : (g + 1) * LANES, j * LANES : (j + 1) * LANES] = jnp.where(
                wanted == j * LANES, 1.0, 0.0
            ).astype(BF16)
    my_loads_ref[...] = jnp.dot(
        pick_ref[...], loads_ref[...], preferred_element_type=F32
    ).astype(BF16)
    my_loads = my_loads_ref[...]
    for influence_ref, out_ref in zip(influence_refs, out_refs):
        share_product(influence_ref, my_loads, out_ref)


def product_kernel(index_ref, my_loads_ref, *refs):
    shares = len(refs) // 2
    my_loads = my_loads_ref[...]
    for influence_ref, out_ref in zip(refs[:shares], refs[shares:]):
        share_product(influence_ref, my_loads, out_ref)


def share_spec(influence, share_rows, which):
    return pl.BlockSpec(
        (influence.shape[0], share_rows, influence.shape[2]),
        lambda i, index_ref: (0, index_ref[which], 0),
    )


def whole_spec(shape):
    return pl.BlockSpec(shape, lambda i, *_: (0,) * len(shape))


def first_products(index, order, loads, influence, share_rows, which):
    components, _, patch_cols = influence.shape
    patches, columns = loads.shape
    share = jax.ShapeDtypeStruct((share_rows, components * columns), BF16)
    out = pl.pallas_call(
        gather_kernel,
        out_shape=[share] * len(which) + [jax.ShapeDtypeStruct((patch_cols, columns), BF16)],
        grid_spec=pltpu.PrefetchScalarGridSpec(
            num_scalar_prefetch=1,
            grid=(1,),
            in_specs=[
                pl.BlockSpec(
                    (1, patch_cols // LANES, LANES), lambda i, index_ref: (index_ref[0], 0, 0)
                ),
                whole_spec(loads.shape),
            ]
            + [share_spec(influence, share_rows, k) for k in which],
            out_specs=[whole_spec(share.shape)] * len(which) + [whole_spec((patch_cols, columns))],
            scratch_shapes=[pltpu.VMEM((patch_cols, patches), BF16)],
        ),
        compiler_params=params(),
        name="first_products",
    )(index, order, loads, *([influence] * len(which)))
    return out[:-1], out[-1]


def more_products(index, my_loads, influence, share_rows, which, kinds):
    components, _, _ = influence.shape
    columns = my_loads.shape[1]
    shape = (share_rows, components * columns)
    return pl.pallas_call(
        product_kernel,
        out_shape=[jax.ShapeDtypeStruct(shape, kind) for kind in kinds],
        grid_spec=pltpu.PrefetchScalarGridSpec(
            num_scalar_prefetch=1,
            grid=(1,),
            in_specs=[whole_spec(my_loads.shape)]
            + [share_spec(influence, share_rows, k) for k in which],
            out_specs=[whole_spec(shape)] * len(which),
        ),
        compiler_params=params(),
        name="more_products",
    )(index, my_loads, *([influence] * len(which)))


def sum_kernel(own_ref, *refs):
    total = own_ref[...]
    for ref in refs[:-1]:
        total = total + ref[...].astype(F32)
    refs[-1][...] = total.astype(BF16)


def share_sum(own, others):
    return pl.pallas_call(
        sum_kernel,
        out_shape=jax.ShapeDtypeStruct(own.shape, BF16),
        compiler_params=pltpu.CompilerParams(vmem_limit_bytes=VMEM_BYTES),
        name="share_sum",
    )(own, *others)


def pick_rows(position_row, block):
    rows = position_row.shape[1]
    wanted = lax.broadcasted_iota(jnp.int32, (BLK, rows), 0) + block * BLK
    return jnp.where(position_row == wanted, 1.0, 0.0).astype(BF16)


def early_kernel(count, pairs_ref, place_ref, position_ref, *refs):
    pieces, out_ref = refs[:-1], refs[-1]
    for s in range(count):
        block = pairs_ref[s // 2, s % 2]
        total = None
        for i, piece in enumerate(pieces):
            pick = pick_rows(position_ref[place_ref[i]], block)
            term = jnp.dot(pick, piece[...], preferred_element_type=F32)
            total = term if total is None else total + term
        out_ref[s] = total


def early_rows(pairs, place, position, pieces):
    count = pairs.shape[0] * 2
    width = pieces[0].shape[1]
    return pl.pallas_call(
        functools.partial(early_kernel, count),
        out_shape=jax.ShapeDtypeStruct((count, BLK, width), F32),
        grid_spec=pltpu.PrefetchScalarGridSpec(
            num_scalar_prefetch=2,
            grid=(1,),
            in_specs=[whole_spec(position.shape)] + [whole_spec(p.shape) for p in pieces],
            out_specs=whole_spec((count, BLK, width)),
        ),
        compiler_params=params(),
        name="early_rows",
    )(pairs, place, position, *pieces)


def cross_kernel(components, pairs_ref, place_ref, position_ref, weights_ref, early_ref, *refs):
    pieces, (out_ref, left_ref, right_ref) = refs[:-3], refs[-3:]
    q = pl.program_id(0)
    columns = weights_ref.shape[1]
    for side, rows_ref in ((0, left_ref), (1, right_ref)):
        block = pairs_ref[q, side]
        total = early_ref[side]
        for i, piece in enumerate(pieces):
            pick = pick_rows(position_ref[place_ref[i]], block)
            total = total + jnp.dot(pick, piece[...], preferred_element_type=F32)
        for c in range(components):
            rows_ref[pl.ds(c, BLK, stride=components), :] = total[:, c * columns : (c + 1) * columns]
    scaled = (left_ref[...] * weights_ref[...]).astype(BF16)
    right = right_ref[...]
    lane = lax.broadcasted_iota(jnp.int32, right.shape, 1)
    turned = pltpu.roll(right, columns // 2, 1)
    turned = jnp.where(lane < columns // 2, -turned, turned)
    for part, other in ((0, right), (1, turned)):
        out_ref[0, part] = lax.dot_general(
            scaled, other.astype(BF16), (((1,), (1,)), ((), ())), preferred_element_type=F32
        ).astype(BF16)


def cross(pairs, place, position, weights, early, pieces, components):
    count = pairs.shape[0]
    columns = weights.shape[1]
    rows = BLK * components
    return pl.pallas_call(
        functools.partial(cross_kernel, components),
        out_shape=jax.ShapeDtypeStruct((count, 2, rows, rows), BF16),
        grid_spec=pltpu.PrefetchScalarGridSpec(
            num_scalar_prefetch=2,
            grid=(count,),
            in_specs=[
                whole_spec(position.shape),
                whole_spec(weights.shape),
                pl.BlockSpec((2,) + early.shape[1:], lambda i, *_: (i, 0, 0)),
            ]
            + [whole_spec(p.shape) for p in pieces],
            out_specs=pl.BlockSpec((1, 2, rows, rows), lambda i, *_: (i, 0, 0, 0)),
            scratch_shapes=[pltpu.VMEM((rows, columns), F32)] * 2,
        ),
        compiler_params=params(),
        name="cross",
    )(pairs, place, position, weights, early, *pieces)


def shards(influence, loads, patch_order, spectral_weights, block_position, block_pairs):
    components, hot_rows, patch_cols = influence.shape
    n_patch, n_hot = lax.axis_size("patch"), lax.axis_size("hot")
    patch_index, hot_index = lax.axis_index("patch"), lax.axis_index("hot")
    share_rows = hot_rows // n_patch
    weights = jnp.concatenate([spectral_weights, spectral_weights])[None, :]
    order = patch_order.reshape(n_patch, patch_cols // LANES, LANES)

    def swap(array, axis, k):
        size = lax.axis_size(axis)
        return lax.ppermute(array, axis, [(i, i ^ k) for i in range(size)])

    index = patch_index ^ jnp.arange(n_patch, dtype=jnp.int32)
    far = list(range(n_patch - 1, n_patch // 2 - 1, -1))
    near = list(range(n_patch // 2 - 1, -1, -1))
    far_terms, my_loads = first_products(index, order, loads, influence, share_rows, far)
    near_terms = more_products(
        index, my_loads, influence, share_rows, near, [BF16] * (len(near) - 1) + [F32]
    )
    received = [swap(t, "patch", k) for k, t in zip(far + near, list(far_terms) + list(near_terms[:-1]))]
    own = share_sum(near_terms[-1], received)

    column = {(0, k): swap(own, "patch", k) if k else own for k in [0] + far + near[:-1]}
    chips = [2 * i for i in range(n_hot // 2)]
    plane = {(j, k): swap(column[0, k], "hot", j) if j else column[0, k] for j in chips for k in range(n_patch)}
    pieces = dict(plane)
    pieces.update({(j + 1, k): swap(piece, "hot", 1) for (j, k), piece in plane.items()})
    late_keys = [(j, k) for j, k in pieces if j >= 2 and k in far]
    early_keys = [key for key in pieces if key not in late_keys]
    position = block_position.reshape(n_hot * n_patch, 1, share_rows)

    def places(keys):
        return jnp.stack([(hot_index ^ j) * n_patch + (patch_index ^ k) for j, k in keys])

    early = early_rows(block_pairs, places(early_keys), position, [pieces[key] for key in early_keys])
    return cross(
        block_pairs, places(late_keys), position, weights, early,
        [pieces[key] for key in late_keys], components,
    )


def solution(mesh):
    placed = (
        P(None, "hot", "patch"),
        P("grp", None),
        P(),
        P("grp"),
        P(),
        P(("hot", "patch"), None),
    )
    return jax.shard_map(
        shards,
        mesh=mesh,
        in_specs=placed,
        out_specs=P(("grp", "hot", "patch"), None, None, None),
        check_vma=False,
    )
```

```python
import functools
import math

import jax
import jax.numpy as jnp
from jax import lax
from jax.experimental import pallas as pl
from jax.experimental.pallas import tpu as pltpu
from jax.sharding import PartitionSpec as P

BLK = 256
LANES = 128
F32 = jnp.float32
BF16 = jnp.bfloat16
VMEM_BYTES = 48 * 1024 * 1024
FIRST_VMEM_BYTES = 125 * 512 * 1024


def params(steps=1):
    return pltpu.CompilerParams(
        dimension_semantics=("arbitrary",) * steps, vmem_limit_bytes=VMEM_BYTES
    )


def cost(flops, bytes_accessed):
    return pl.CostEstimate(flops=flops, bytes_accessed=bytes_accessed, transcendentals=0)


def products(influence, my_loads, out_refs):
    shares, components, rows, patch_cols = influence.shape
    columns = my_loads.shape[1]
    part = jnp.dot(
        influence.reshape(shares * components * rows, patch_cols), my_loads,
        preferred_element_type=F32,
    )
    for i, out_ref in enumerate(out_refs):
        for c in range(components):
            top = (i * components + c) * rows
            out_ref[:, c * columns : (c + 1) * columns] = part[top : top + rows].astype(out_ref.dtype)


def share_copies(influence_ref, held_ref, sems, which):
    rows = held_ref.shape[2]
    here = lax.axis_index("patch")
    return [
        pltpu.make_async_copy(
            influence_ref.at[:, pl.ds(pl.multiple_of((here ^ k) * rows, rows), rows), :],
            held_ref.at[i],
            sems.at[i],
        )
        for i, k in enumerate(which)
    ]


def first_kernel(which, order_ref, loads_ref, influence_ref, *refs):
    out_refs, (my_loads_ref, own_order, column_ref, table, pick_ref, held, sems) = refs[:-7], refs[-7:]
    columns = loads_ref.shape[1]
    half = loads_ref.shape[0] // 2
    order_copy = pltpu.make_async_copy(order_ref.at[lax.axis_index("patch")], own_order, sems.at[0])
    low_copy = pltpu.make_async_copy(
        loads_ref.at[pl.ds(0, half)], table.at[:, pl.ds(0, columns)], sems.at[1]
    )
    high_copy = pltpu.make_async_copy(
        loads_ref.at[pl.ds(half, half)], table.at[:, pl.ds(columns, columns)], sems.at[2]
    )
    copies = share_copies(influence_ref, held, sems.at[pl.ds(3, len(which))], which)
    order_copy.start()
    low_copy.start()
    high_copy.start()
    for copy in copies:
        copy.start()
    order_copy.wait()
    lane = lax.broadcasted_iota(jnp.int32, (LANES, LANES), 1)
    for g in range(own_order.shape[0]):
        rows = slice(g * LANES, (g + 1) * LANES)
        wanted = jnp.transpose(jnp.broadcast_to(own_order[g : g + 1, :], (LANES, LANES)))
        column_ref[rows, :] = wanted
        wanted = jnp.where(wanted >= half, wanted - half, wanted) - lane
        for j in range(half // LANES):
            pick_ref[rows, j * LANES : (j + 1) * LANES] = jnp.where(
                wanted == j * LANES, 1.0, 0.0
            ).astype(BF16)
    low_copy.wait()
    high_copy.wait()
    both = jnp.dot(pick_ref[...], table[...], preferred_element_type=F32)
    my_loads_ref[...] = jnp.where(
        column_ref[...] >= half, both[:, columns:], both[:, :columns]
    ).astype(BF16)
    for copy in copies:
        copy.wait()
    products(held[...], my_loads_ref[...], out_refs)


def more_kernel(which, my_loads_ref, influence_ref, *refs):
    out_refs, (held, sems) = refs[:-2], refs[-2:]
    copies = share_copies(influence_ref, held, sems, which)
    for copy in copies:
        copy.start()
    for copy in copies:
        copy.wait()
    products(held[...], my_loads_ref[...], out_refs)


def vmem():
    return pl.BlockSpec(memory_space=pltpu.VMEM)


def hbm():
    return pl.BlockSpec(memory_space=pltpu.HBM)


def first_products(order, loads, influence, share_rows, which):
    components, _, patch_cols = influence.shape
    patches, columns = loads.shape
    share = jax.ShapeDtypeStruct((share_rows, components * columns), BF16)
    held = (len(which), components, share_rows, patch_cols)
    out = pl.pallas_call(
        functools.partial(first_kernel, which),
        out_shape=[share] * len(which) + [jax.ShapeDtypeStruct((patch_cols, columns), BF16)],
        in_specs=[hbm()] * 3,
        out_specs=[vmem()] * (len(which) + 1),
        scratch_shapes=[
            pltpu.VMEM(order.shape[1:], jnp.int32),
            pltpu.VMEM((patch_cols, columns), jnp.int32),
            pltpu.VMEM((patches // 2, 2 * columns), BF16),
            pltpu.VMEM((patch_cols, patches // 2), BF16),
            pltpu.VMEM(held, BF16),
            pltpu.SemaphoreType.DMA((3 + len(which),)),
        ],
        compiler_params=pltpu.CompilerParams(vmem_limit_bytes=FIRST_VMEM_BYTES),
        name="first_products",
    )(order, loads, influence)
    return out[:-1], out[-1]


def more_products(my_loads, influence, share_rows, which, kinds):
    components, _, patch_cols = influence.shape
    columns = my_loads.shape[1]
    shape = (share_rows, components * columns)
    held = (len(which), components, share_rows, patch_cols)
    return pl.pallas_call(
        functools.partial(more_kernel, which),
        out_shape=[jax.ShapeDtypeStruct(shape, kind) for kind in kinds],
        in_specs=[vmem(), hbm()],
        out_specs=[vmem()] * len(which),
        scratch_shapes=[pltpu.VMEM(held, BF16), pltpu.SemaphoreType.DMA((len(which),))],
        compiler_params=pltpu.CompilerParams(vmem_limit_bytes=VMEM_BYTES),
        cost_estimate=cost(8 * share_rows * components * columns * patch_cols, 8 * math.prod(held)),
        name="more_products",
    )(my_loads, influence)


def sum_kernel(own_ref, *refs):
    total = own_ref[...]
    for ref in refs[:-1]:
        total = total + ref[...].astype(F32)
    refs[-1][...] = total.astype(BF16)


def share_sum(own, others):
    return pl.pallas_call(
        sum_kernel,
        out_shape=jax.ShapeDtypeStruct(own.shape, BF16),
        compiler_params=pltpu.CompilerParams(vmem_limit_bytes=VMEM_BYTES),
        name="share_sum",
    )(own, *others)


def pick_rows(position_ref, key, block):
    n_patch = lax.axis_size("patch")
    place = (lax.axis_index("hot") ^ key[0]) * n_patch + (lax.axis_index("patch") ^ key[1])
    rows = position_ref.shape[2]
    wanted = lax.broadcasted_iota(jnp.int32, (BLK, rows), 0) + block * BLK
    return jnp.where(position_ref[place] == wanted, 1.0, 0.0).astype(BF16)


def early_kernel(keys, pairs_ref, position_ref, *refs):
    pieces, befores, out_ref = refs[: len(keys)], refs[len(keys) : -1], refs[-1]
    for s in range(out_ref.shape[0]):
        block = pairs_ref[s // 2, s % 2]
        total = befores[0][s] if befores else None
        for key, piece in zip(keys, pieces):
            pick = pick_rows(position_ref, key, block)
            term = jnp.dot(pick, piece[...], preferred_element_type=F32)
            total = term if total is None else total + term
        out_ref[s] = total


def early_rows(pairs, position, keys, pieces, before=()):
    count = pairs.shape[0] * 2
    rows, width = pieces[0].shape
    flops = 2 * count * BLK * rows * width * len(keys)
    return pl.pallas_call(
        functools.partial(early_kernel, keys),
        out_shape=jax.ShapeDtypeStruct((count, BLK, width), F32),
        in_specs=[pl.BlockSpec(memory_space=pltpu.SMEM)] + [vmem()] * (1 + len(pieces) + len(before)),
        out_specs=vmem(),
        compiler_params=pltpu.CompilerParams(vmem_limit_bytes=VMEM_BYTES),
        cost_estimate=cost(2 * flops, 8 * count * BLK * width),
        name="early_rows",
    )(pairs, position, *pieces, *before)


def cross_kernel(components, keys, pairs_ref, position_ref, weights_ref, early_ref, *refs):
    pieces, (out_ref, left_ref, right_ref) = refs[:-3], refs[-3:]
    q = pl.program_id(0)
    columns = weights_ref.shape[1]
    for side, rows_ref in ((0, left_ref), (1, right_ref)):
        block = pairs_ref[q, side]
        total = early_ref[side]
        for key, piece in zip(keys, pieces):
            pick = pick_rows(position_ref, key, block)
            total = total + jnp.dot(pick, piece[...], preferred_element_type=F32)
        for c in range(components):
            rows_ref[pl.ds(c, BLK, stride=components), :] = total[:, c * columns : (c + 1) * columns]
    scaled = (left_ref[...] * weights_ref[...]).astype(BF16)
    right = right_ref[...]
    lane = lax.broadcasted_iota(jnp.int32, right.shape, 1)
    turned = pltpu.roll(right, columns // 2, 1)
    turned = jnp.where(lane < columns // 2, -turned, turned)
    for part, other in ((0, right), (1, turned)):
        out_ref[0, part] = lax.dot_general(
            scaled, other.astype(BF16), (((1,), (1,)), ((), ())), preferred_element_type=F32
        ).astype(BF16)


def cross(pairs, position, weights, early, keys, pieces, components):
    count = pairs.shape[0]
    columns = weights.shape[1]
    rows = BLK * components
    return pl.pallas_call(
        functools.partial(cross_kernel, components, keys),
        out_shape=jax.ShapeDtypeStruct((count, 2, rows, rows), BF16),
        grid=(count,),
        in_specs=[
            pl.BlockSpec(memory_space=pltpu.SMEM),
            vmem(),
            vmem(),
            pl.BlockSpec((2,) + early.shape[1:], lambda i: (i, 0, 0)),
        ]
        + [vmem()] * len(pieces),
        out_specs=pl.BlockSpec((1, 2, rows, rows), lambda i: (i, 0, 0, 0)),
        scratch_shapes=[pltpu.VMEM((rows, columns), F32)] * 2,
        compiler_params=params(),
        name="cross",
    )(pairs, position, weights, early, *pieces)


def gather_plane(own, swap, n_patch, n_hot):
    plane = {(0, 0): own}
    bits = [1 << b for b in reversed(range((n_patch - 1).bit_length()))]
    for bit in bits:
        for _, k in list(plane):
            plane[0, k ^ bit] = swap(plane[0, k], "patch", bit)
    chip_bits = [2 << b for b in reversed(range((n_hot // 2 - 1).bit_length()))]
    for bit in chip_bits:
        for j, k in list(plane):
            if k != n_patch - 1:
                plane[j ^ bit, k] = swap(plane[j, k], "hot", bit)
    for j in range(2, n_hot, 2):
        plane[j, n_patch - 1] = swap(plane[j, 0], "patch", n_patch - 1)
    return plane


def shards(influence, loads, patch_order, spectral_weights, block_position, block_pairs):
    components, hot_rows, patch_cols = influence.shape
    n_patch, n_hot = lax.axis_size("patch"), lax.axis_size("hot")
    share_rows = hot_rows // n_patch
    weights = jnp.concatenate([spectral_weights, spectral_weights])[None, :]
    order = patch_order.reshape(n_patch, patch_cols // LANES, LANES)

    def swap(array, axis, k):
        size = lax.axis_size(axis)
        return lax.ppermute(array, axis, [(i, i ^ k) for i in range(size)])

    far = list(range(n_patch - 1, n_patch // 2 - 1, -1))
    near = list(range(n_patch // 2 - 1, -1, -1))
    far_terms, my_loads = first_products(order, loads, influence, share_rows, far)
    near_terms = more_products(
        my_loads, influence, share_rows, near, [BF16] * (len(near) - 1) + [F32]
    )
    received = [swap(t, "patch", k) for k, t in zip(far + near, list(far_terms) + list(near_terms[:-1]))]
    own = share_sum(near_terms[-1], received)

    plane = gather_plane(own, swap, n_patch, n_hot)
    pieces = dict(plane)
    pieces.update({(j + 1, k): swap(piece, "hot", 1) for (j, k), piece in plane.items()})
    position = block_position.reshape(n_hot * n_patch, 1, share_rows)
    late = [key for key in pieces if key[0] >= 2 and key[1] in far]
    first = [key for key in pieces if (key[0] < 2 and key[1] not in far) or key[1] == 0]
    second = [key for key in pieces if key not in late and key not in first]
    early = early_rows(block_pairs, position, first, [pieces[key] for key in first])
    early = early_rows(block_pairs, position, second, [pieces[key] for key in second], [early])
    return cross(
        block_pairs, position, weights, early, late, [pieces[key] for key in late], components
    )


def solution(mesh):
    placed = (
        P(None, "hot", "patch"),
        P("grp", None),
        P(),
        P("grp"),
        P(),
        P(("hot", "patch"), None),
    )
    return jax.shard_map(
        shards,
        mesh=mesh,
        in_specs=placed,
        out_specs=P(("grp", "hot", "patch"), None, None, None),
        check_vma=False,
    )
```

```python
import functools
import math

import jax
import jax.numpy as jnp
from jax import lax
from jax.experimental import pallas as pl
from jax.experimental.pallas import tpu as pltpu
from jax.sharding import PartitionSpec as P

BLK = 256
LANES = 128
F32 = jnp.float32
BF16 = jnp.bfloat16
VMEM_BYTES = 48 * 1024 * 1024
FIRST_VMEM_BYTES = 124 * 512 * 1024


def params(steps=1):
    return pltpu.CompilerParams(
        dimension_semantics=("arbitrary",) * steps, vmem_limit_bytes=VMEM_BYTES
    )


def cost(flops, bytes_accessed):
    return pl.CostEstimate(flops=flops, bytes_accessed=bytes_accessed, transcendentals=0)


def products(influence, my_loads, out_refs):
    shares, components, rows, patch_cols = influence.shape
    columns = my_loads.shape[1]
    part = jnp.dot(
        influence.reshape(shares * components * rows, patch_cols), my_loads,
        preferred_element_type=F32,
    )
    for i, out_ref in enumerate(out_refs):
        for c in range(components):
            top = (i * components + c) * rows
            out_ref[:, c * columns : (c + 1) * columns] = part[top : top + rows].astype(out_ref.dtype)


def share_copies(influence_ref, held_ref, sems, which):
    rows = held_ref.shape[2]
    here = lax.axis_index("patch")
    return [
        pltpu.make_async_copy(
            influence_ref.at[:, pl.ds(pl.multiple_of((here ^ k) * rows, rows), rows), :],
            held_ref.at[i],
            sems.at[i],
        )
        for i, k in enumerate(which)
    ]


def first_kernel(which, order_ref, loads_ref, influence_ref, *refs):
    out_refs, (my_loads_ref, own_order, column_ref, table, pick_ref, held, sems) = refs[:-7], refs[-7:]
    columns = loads_ref.shape[1]
    half = loads_ref.shape[0] // 2
    order_copy = pltpu.make_async_copy(order_ref.at[lax.axis_index("patch")], own_order, sems.at[0])
    low_copy = pltpu.make_async_copy(
        loads_ref.at[pl.ds(0, half)], table.at[:, pl.ds(0, columns)], sems.at[1]
    )
    high_copy = pltpu.make_async_copy(
        loads_ref.at[pl.ds(half, half)], table.at[:, pl.ds(columns, columns)], sems.at[2]
    )
    copies = share_copies(influence_ref, held, sems.at[pl.ds(3, len(which))], which)
    order_copy.start()
    low_copy.start()
    high_copy.start()
    for copy in copies:
        copy.start()
    order_copy.wait()
    lane = lax.broadcasted_iota(jnp.int32, (LANES, LANES), 1)
    for g in range(own_order.shape[0]):
        rows = slice(g * LANES, (g + 1) * LANES)
        wanted = jnp.transpose(jnp.broadcast_to(own_order[g : g + 1, :], (LANES, LANES)))
        column_ref[rows, :] = wanted
        wanted = jnp.where(wanted >= half, wanted - half, wanted) - lane
        for j in range(half // LANES):
            pick_ref[rows, j * LANES : (j + 1) * LANES] = jnp.where(
                wanted == j * LANES, 1.0, 0.0
            ).astype(BF16)
    low_copy.wait()
    high_copy.wait()
    both = jnp.dot(pick_ref[...], table[...], preferred_element_type=F32)
    my_loads_ref[...] = jnp.where(
        column_ref[...] >= half, both[:, columns:], both[:, :columns]
    ).astype(BF16)
    for copy in copies:
        copy.wait()
    products(held[...], my_loads_ref[...], out_refs)


def more_kernel(which, my_loads_ref, influence_ref, *refs):
    out_refs, (held, sems) = refs[:-2], refs[-2:]
    copies = share_copies(influence_ref, held, sems, which)
    for copy in copies:
        copy.start()
    for copy in copies:
        copy.wait()
    products(held[...], my_loads_ref[...], out_refs)


def vmem():
    return pl.BlockSpec(memory_space=pltpu.VMEM)


def hbm():
    return pl.BlockSpec(memory_space=pltpu.HBM)


def first_products(order, loads, influence, share_rows, which):
    components, _, patch_cols = influence.shape
    patches, columns = loads.shape
    share = jax.ShapeDtypeStruct((share_rows, components * columns), BF16)
    held = (len(which), components, share_rows, patch_cols)
    out = pl.pallas_call(
        functools.partial(first_kernel, which),
        out_shape=[share] * len(which) + [jax.ShapeDtypeStruct((patch_cols, columns), BF16)],
        in_specs=[hbm()] * 3,
        out_specs=[vmem()] * (len(which) + 1),
        scratch_shapes=[
            pltpu.VMEM(order.shape[1:], jnp.int32),
            pltpu.VMEM((patch_cols, columns), jnp.int32),
            pltpu.VMEM((patches // 2, 2 * columns), BF16),
            pltpu.VMEM((patch_cols, patches // 2), BF16),
            pltpu.VMEM(held, BF16),
            pltpu.SemaphoreType.DMA((3 + len(which),)),
        ],
        compiler_params=pltpu.CompilerParams(vmem_limit_bytes=FIRST_VMEM_BYTES),
        name="first_products",
    )(order, loads, influence)
    return out[:-1], out[-1]


def more_products(my_loads, influence, share_rows, which, kinds):
    components, _, patch_cols = influence.shape
    columns = my_loads.shape[1]
    shape = (share_rows, components * columns)
    held = (len(which), components, share_rows, patch_cols)
    return pl.pallas_call(
        functools.partial(more_kernel, which),
        out_shape=[jax.ShapeDtypeStruct(shape, kind) for kind in kinds],
        in_specs=[vmem(), hbm()],
        out_specs=[vmem()] * len(which),
        scratch_shapes=[pltpu.VMEM(held, BF16), pltpu.SemaphoreType.DMA((len(which),))],
        compiler_params=pltpu.CompilerParams(vmem_limit_bytes=VMEM_BYTES),
        cost_estimate=cost(8 * share_rows * components * columns * patch_cols, 8 * math.prod(held)),
        name="more_products",
    )(my_loads, influence)


def sum_kernel(own_ref, *refs):
    total = own_ref[...]
    for ref in refs[:-1]:
        total = total + ref[...].astype(F32)
    refs[-1][...] = total.astype(BF16)


def share_sum(own, others):
    return pl.pallas_call(
        sum_kernel,
        out_shape=jax.ShapeDtypeStruct(own.shape, BF16),
        compiler_params=pltpu.CompilerParams(vmem_limit_bytes=VMEM_BYTES),
        name="share_sum",
    )(own, *others)


def pick_rows(position_ref, key, block):
    n_patch = lax.axis_size("patch")
    place = (lax.axis_index("hot") ^ key[0]) * n_patch + (lax.axis_index("patch") ^ key[1])
    rows = position_ref.shape[2]
    offset = position_ref[place] - block * BLK
    return jnp.where(offset == lax.broadcasted_iota(jnp.int32, (BLK, rows), 0), 1.0, 0.0).astype(BF16)


def early_kernel(keys, pairs_ref, position_ref, *refs):
    pieces, befores, (out_ref, joined_ref) = refs[: len(keys)], refs[len(keys) : -2], refs[-2:]
    rows = pieces[0].shape[0]
    for i, piece in enumerate(pieces):
        joined_ref[i * rows : (i + 1) * rows, :] = piece[...]
    for s in range(out_ref.shape[0]):
        block = pairs_ref[s // 2, s % 2]
        pick = jnp.concatenate([pick_rows(position_ref, key, block) for key in keys], axis=1)
        total = jnp.dot(pick, joined_ref[...], preferred_element_type=F32)
        out_ref[s] = total + befores[0][s] if befores else total


def early_rows(pairs, position, keys, pieces, before=()):
    count = pairs.shape[0] * 2
    rows, width = pieces[0].shape
    flops = 2 * count * BLK * rows * width * len(keys)
    return pl.pallas_call(
        functools.partial(early_kernel, keys),
        out_shape=jax.ShapeDtypeStruct((count, BLK, width), F32),
        in_specs=[pl.BlockSpec(memory_space=pltpu.SMEM)] + [vmem()] * (1 + len(pieces) + len(before)),
        out_specs=vmem(),
        scratch_shapes=[pltpu.VMEM((len(keys) * rows, width), BF16)],
        compiler_params=pltpu.CompilerParams(vmem_limit_bytes=VMEM_BYTES),
        cost_estimate=cost(2 * flops, 8 * count * BLK * width),
        name="early_rows",
    )(pairs, position, *pieces, *before)


def cross_kernel(components, keys, pairs_ref, position_ref, weights_ref, early_ref, *refs):
    pieces, (out_ref, left_ref, right_ref) = refs[:-3], refs[-3:]
    q = pl.program_id(0)
    columns = weights_ref.shape[1]
    for side, rows_ref in ((0, left_ref), (1, right_ref)):
        block = pairs_ref[q, side]
        total = early_ref[side]
        for key, piece in zip(keys, pieces):
            pick = pick_rows(position_ref, key, block)
            total = total + jnp.dot(pick, piece[...], preferred_element_type=F32)
        for c in range(components):
            rows_ref[pl.ds(c, BLK, stride=components), :] = total[:, c * columns : (c + 1) * columns]
    scaled = (left_ref[...] * weights_ref[...]).astype(BF16)
    right = right_ref[...]
    lane = lax.broadcasted_iota(jnp.int32, right.shape, 1)
    turned = pltpu.roll(right, columns // 2, 1)
    turned = jnp.where(lane < columns // 2, -turned, turned)
    for part, other in ((0, right), (1, turned)):
        out_ref[0, part] = lax.dot_general(
            scaled, other.astype(BF16), (((1,), (1,)), ((), ())), preferred_element_type=F32
        ).astype(BF16)


def cross(pairs, position, weights, early, keys, pieces, components):
    count = pairs.shape[0]
    columns = weights.shape[1]
    rows = BLK * components
    return pl.pallas_call(
        functools.partial(cross_kernel, components, keys),
        out_shape=jax.ShapeDtypeStruct((count, 2, rows, rows), BF16),
        grid=(count,),
        in_specs=[
            pl.BlockSpec(memory_space=pltpu.SMEM),
            vmem(),
            vmem(),
            pl.BlockSpec((2,) + early.shape[1:], lambda i: (i, 0, 0)),
        ]
        + [vmem()] * len(pieces),
        out_specs=pl.BlockSpec((1, 2, rows, rows), lambda i: (i, 0, 0, 0)),
        scratch_shapes=[pltpu.VMEM((rows, columns), F32)] * 2,
        compiler_params=params(),
        name="cross",
    )(pairs, position, weights, early, *pieces)


def shards(influence, loads, patch_order, spectral_weights, block_position, block_pairs):
    components, hot_rows, patch_cols = influence.shape
    n_patch, n_hot = lax.axis_size("patch"), lax.axis_size("hot")
    share_rows = hot_rows // n_patch
    weights = jnp.concatenate([spectral_weights, spectral_weights])[None, :]
    order = patch_order.reshape(n_patch, patch_cols // LANES, LANES)

    def swap(array, axis, k):
        size = lax.axis_size(axis)
        return lax.ppermute(array, axis, [(i, i ^ k) for i in range(size)])

    far = list(range(n_patch - 1, n_patch // 2 - 1, -1))
    near = list(range(n_patch // 2 - 1, -1, -1))
    far_terms, my_loads = first_products(order, loads, influence, share_rows, far)
    near_terms = more_products(
        my_loads, influence, share_rows, near, [BF16] * (len(near) - 1) + [F32]
    )
    received = [swap(t, "patch", k) for k, t in zip(far + near, list(far_terms) + list(near_terms[:-1]))]
    own = share_sum(near_terms[-1], received)

    position = block_position.reshape(n_hot * n_patch, 1, share_rows)
    top = n_patch // 2
    patch_bits = [1 << b for b in reversed(range((n_patch - 1).bit_length()))]
    chip_bits = [2 << b for b in reversed(range((n_hot // 2 - 1).bit_length()))]
    tie = lambda value, *after: lax.optimization_barrier((value, *after))[0]

    plane, pieces = {(0, 0): own}, {}

    def along(keys, axis, bits):
        for bit in bits:
            for j, k in list(keys):
                key = (j ^ bit, k) if axis == "hot" else (j, k ^ bit)
                plane[key] = swap(plane[j, k], axis, bit)
                keys = keys + [key]
        return keys

    def cores(keys):
        for j, k in keys:
            pieces[j, k] = plane[j, k]
            pieces[j + 1, k] = swap(plane[j, k], "hot", 1)
        return [(j + c, k) for j, k in keys for c in (0, 1)]

    def picked(keys, *before):
        return early_rows(block_pairs, position, keys, [pieces[key] for key in keys], before)

    head = cores([(0, 0)])
    along([(0, 0)], "patch", patch_bits[:1])
    near_keys = along([(0, 0)], "patch", patch_bits[1:])
    chip_keys = along([(0, 0)], "hot", chip_bits)
    for key in near_keys[1:] + chip_keys[1:]:
        plane[key] = tie(plane[key], plane[0, top])
    far_keys = along([(0, top)], "patch", patch_bits[1:])
    for j, _ in chip_keys[1:]:
        plane[j, n_patch - 1] = swap(plane[j, 0], "patch", n_patch - 1)
    early = picked(head + cores(near_keys[1:] + chip_keys[1:] + [(0, top)]))
    later = []
    for key in near_keys[1:] + far_keys[:-1]:
        later += along([key], "hot", chip_bits)[1:]
    middle = [key for key in later if key[1] < top]
    early = picked(cores(far_keys[1:] + middle), early)
    last = [key for key in plane if key not in pieces]
    for key in last:
        plane[key] = tie(plane[key], early)
    late = cores(last)
    return cross(
        block_pairs, position, weights, early, late, [pieces[key] for key in late], components
    )


def solution(mesh):
    placed = (
        P(None, "hot", "patch"),
        P("grp", None),
        P(),
        P("grp"),
        P(),
        P(("hot", "patch"), None),
    )
    return jax.shard_map(
        shards,
        mesh=mesh,
        in_specs=placed,
        out_specs=P(("grp", "hot", "patch"), None, None, None),
        check_vma=False,
    )
```

```python
import functools
import math

import jax
import jax.numpy as jnp
from jax import lax
from jax.experimental import pallas as pl
from jax.experimental.pallas import tpu as pltpu
from jax.sharding import PartitionSpec as P

BLK = 256
LANES = 128
F32 = jnp.float32
BF16 = jnp.bfloat16
VMEM_BYTES = 48 * 1024 * 1024
FIRST_VMEM_BYTES = 124 * 512 * 1024


def params(steps=1):
    return pltpu.CompilerParams(
        dimension_semantics=("arbitrary",) * steps, vmem_limit_bytes=VMEM_BYTES
    )


def cost(flops, bytes_accessed):
    return pl.CostEstimate(flops=flops, bytes_accessed=bytes_accessed, transcendentals=0)


def products(influence, my_loads, out_refs):
    shares, components, rows, patch_cols = influence.shape
    columns = my_loads.shape[1]
    part = jnp.dot(
        influence.reshape(shares * components * rows, patch_cols), my_loads,
        preferred_element_type=F32,
    )
    for i, out_ref in enumerate(out_refs):
        for c in range(components):
            top = (i * components + c) * rows
            out_ref[:, c * columns : (c + 1) * columns] = part[top : top + rows].astype(out_ref.dtype)


def share_copies(influence_ref, held_ref, sems, which):
    rows = held_ref.shape[2]
    here = lax.axis_index("patch")
    return [
        pltpu.make_async_copy(
            influence_ref.at[:, pl.ds(pl.multiple_of((here ^ k) * rows, rows), rows), :],
            held_ref.at[i],
            sems.at[i],
        )
        for i, k in enumerate(which)
    ]


def first_kernel(which, order_ref, loads_ref, influence_ref, *refs):
    out_refs, (my_loads_ref, own_order, column_ref, table, pick_ref, held, sems) = refs[:-7], refs[-7:]
    columns = loads_ref.shape[1]
    half = loads_ref.shape[0] // 2
    order_copy = pltpu.make_async_copy(order_ref.at[lax.axis_index("patch")], own_order, sems.at[0])
    low_copy = pltpu.make_async_copy(
        loads_ref.at[pl.ds(0, half)], table.at[:, pl.ds(0, columns)], sems.at[1]
    )
    high_copy = pltpu.make_async_copy(
        loads_ref.at[pl.ds(half, half)], table.at[:, pl.ds(columns, columns)], sems.at[2]
    )
    copies = share_copies(influence_ref, held, sems.at[pl.ds(3, len(which))], which)
    order_copy.start()
    low_copy.start()
    high_copy.start()
    for copy in copies:
        copy.start()
    order_copy.wait()
    lane = lax.broadcasted_iota(jnp.int32, (LANES, LANES), 1)
    low_copy.wait()
    high_copy.wait()
    for g in range(own_order.shape[0] * LANES // 512):
        wanteds = []
        for h in range(512 // LANES):
            i = g * (512 // LANES) + h
            wanteds.append(jnp.transpose(jnp.broadcast_to(own_order[i : i + 1, :], (LANES, LANES))))
        wanted = jnp.concatenate(wanteds, axis=0)
        low = jnp.where(wanted >= half, wanted - half, wanted) - lax.broadcasted_iota(jnp.int32, wanted.shape, 1)
        pick = jnp.concatenate(
            [jnp.where(low == j * LANES, 1.0, 0.0).astype(BF16) for j in range(half // LANES)], axis=1
        )
        both = jnp.dot(pick, table[...], preferred_element_type=F32)
        my_loads_ref[g * 512 : (g + 1) * 512, :] = jnp.where(
            wanted >= half, both[:, columns:], both[:, :columns]
        ).astype(BF16)
    for copy in copies:
        copy.wait()
    products(held[...], my_loads_ref[...], out_refs)


def more_kernel(which, my_loads_ref, influence_ref, *refs):
    out_refs, (held, sems) = refs[:-2], refs[-2:]
    copies = share_copies(influence_ref, held, sems, which)
    for copy in copies:
        copy.start()
    for copy in copies:
        copy.wait()
    products(held[...], my_loads_ref[...], out_refs)


def vmem():
    return pl.BlockSpec(memory_space=pltpu.VMEM)


def hbm():
    return pl.BlockSpec(memory_space=pltpu.HBM)


def first_products(order, loads, influence, share_rows, which):
    components, _, patch_cols = influence.shape
    patches, columns = loads.shape
    share = jax.ShapeDtypeStruct((share_rows, components * columns), BF16)
    held = (len(which), components, share_rows, patch_cols)
    out = pl.pallas_call(
        functools.partial(first_kernel, which),
        out_shape=[share] * len(which) + [jax.ShapeDtypeStruct((patch_cols, columns), BF16)],
        in_specs=[hbm()] * 3,
        out_specs=[vmem()] * (len(which) + 1),
        scratch_shapes=[
            pltpu.VMEM(order.shape[1:], jnp.int32),
            pltpu.VMEM((patch_cols, columns), jnp.int32),
            pltpu.VMEM((patches // 2, 2 * columns), BF16),
            pltpu.VMEM((patch_cols, patches // 2), BF16),
            pltpu.VMEM(held, BF16),
            pltpu.SemaphoreType.DMA((3 + len(which),)),
        ],
        compiler_params=pltpu.CompilerParams(vmem_limit_bytes=FIRST_VMEM_BYTES),
        name="first_products",
    )(order, loads, influence)
    return out[:-1], out[-1]


def more_products(my_loads, influence, share_rows, which, kinds):
    components, _, patch_cols = influence.shape
    columns = my_loads.shape[1]
    shape = (share_rows, components * columns)
    held = (len(which), components, share_rows, patch_cols)
    return pl.pallas_call(
        functools.partial(more_kernel, which),
        out_shape=[jax.ShapeDtypeStruct(shape, kind) for kind in kinds],
        in_specs=[vmem(), hbm()],
        out_specs=[vmem()] * len(which),
        scratch_shapes=[pltpu.VMEM(held, BF16), pltpu.SemaphoreType.DMA((len(which),))],
        compiler_params=pltpu.CompilerParams(vmem_limit_bytes=VMEM_BYTES),
        cost_estimate=cost(8 * share_rows * components * columns * patch_cols, 8 * math.prod(held)),
        name="more_products",
    )(my_loads, influence)


def sum_kernel(own_ref, *refs):
    total = own_ref[...]
    for ref in refs[:-1]:
        total = total + ref[...].astype(F32)
    refs[-1][...] = total.astype(BF16)


def share_sum(own, others):
    return pl.pallas_call(
        sum_kernel,
        out_shape=jax.ShapeDtypeStruct(own.shape, BF16),
        compiler_params=pltpu.CompilerParams(vmem_limit_bytes=VMEM_BYTES),
        name="share_sum",
    )(own, *others)


def pick_rows(position_ref, key, block):
    n_patch = lax.axis_size("patch")
    place = (lax.axis_index("hot") ^ key[0]) * n_patch + (lax.axis_index("patch") ^ key[1])
    rows = position_ref.shape[2]
    offset = position_ref[place] - block * BLK
    return jnp.where(offset == lax.broadcasted_iota(jnp.int32, (BLK, rows), 0), 1.0, 0.0).astype(BF16)


def early_kernel(keys, pairs_ref, position_ref, *refs):
    pieces, befores, (out_ref, joined_ref) = refs[: len(keys)], refs[len(keys) : -2], refs[-2:]
    rows = pieces[0].shape[0]
    for i, piece in enumerate(pieces):
        joined_ref[i * rows : (i + 1) * rows, :] = piece[...]
    for s in range(out_ref.shape[0]):
        block = pairs_ref[s // 2, s % 2]
        pick = jnp.concatenate([pick_rows(position_ref, key, block) for key in keys], axis=1)
        total = jnp.dot(pick, joined_ref[...], preferred_element_type=F32)
        out_ref[s] = total + befores[0][s] if befores else total


def early_rows(pairs, position, keys, pieces, before=()):
    count = pairs.shape[0] * 2
    rows, width = pieces[0].shape
    flops = 2 * count * BLK * rows * width * len(keys)
    return pl.pallas_call(
        functools.partial(early_kernel, keys),
        out_shape=jax.ShapeDtypeStruct((count, BLK, width), F32),
        in_specs=[pl.BlockSpec(memory_space=pltpu.SMEM)] + [vmem()] * (1 + len(pieces) + len(before)),
        out_specs=vmem(),
        scratch_shapes=[pltpu.VMEM((len(keys) * rows, width), BF16)],
        compiler_params=pltpu.CompilerParams(vmem_limit_bytes=VMEM_BYTES),
        cost_estimate=cost(2 * flops, 8 * count * BLK * width),
        name="early_rows",
    )(pairs, position, *pieces, *before)


def cross_kernel(components, keys, pairs_ref, position_ref, weights_ref, early_ref, *refs):
    pieces, (out_ref, left_ref, right_ref) = refs[:-3], refs[-3:]
    q = pl.program_id(0)
    columns = weights_ref.shape[1]
    for side, rows_ref in ((0, left_ref), (1, right_ref)):
        block = pairs_ref[q, side]
        total = early_ref[side]
        for key, piece in zip(keys, pieces):
            pick = pick_rows(position_ref, key, block)
            total = total + jnp.dot(pick, piece[...], preferred_element_type=F32)
        for c in range(components):
            rows_ref[pl.ds(c, BLK, stride=components), :] = total[:, c * columns : (c + 1) * columns]
    scaled = (left_ref[...] * weights_ref[...]).astype(BF16)
    right = right_ref[...]
    lane = lax.broadcasted_iota(jnp.int32, right.shape, 1)
    turned = pltpu.roll(right, columns // 2, 1)
    turned = jnp.where(lane < columns // 2, -turned, turned)
    for part, other in ((0, right), (1, turned)):
        out_ref[0, part] = lax.dot_general(
            scaled, other.astype(BF16), (((1,), (1,)), ((), ())), preferred_element_type=F32
        ).astype(BF16)


def cross(pairs, position, weights, early, keys, pieces, components):
    count = pairs.shape[0]
    columns = weights.shape[1]
    rows = BLK * components
    return pl.pallas_call(
        functools.partial(cross_kernel, components, keys),
        out_shape=jax.ShapeDtypeStruct((count, 2, rows, rows), BF16),
        grid=(count,),
        in_specs=[
            pl.BlockSpec(memory_space=pltpu.SMEM),
            vmem(),
            vmem(),
            pl.BlockSpec((2,) + early.shape[1:], lambda i: (i, 0, 0)),
        ]
        + [vmem()] * len(pieces),
        out_specs=pl.BlockSpec((1, 2, rows, rows), lambda i: (i, 0, 0, 0)),
        scratch_shapes=[pltpu.VMEM((rows, columns), F32)] * 2,
        compiler_params=params(),
        name="cross",
    )(pairs, position, weights, early, *pieces)


def shards(influence, loads, patch_order, spectral_weights, block_position, block_pairs):
    components, hot_rows, patch_cols = influence.shape
    n_patch, n_hot = lax.axis_size("patch"), lax.axis_size("hot")
    share_rows = hot_rows // n_patch
    weights = jnp.concatenate([spectral_weights, spectral_weights])[None, :]
    order = patch_order.reshape(n_patch, patch_cols // LANES, LANES)

    def swap(array, axis, k):
        size = lax.axis_size(axis)
        return lax.ppermute(array, axis, [(i, i ^ k) for i in range(size)])

    far = list(range(n_patch - 1, n_patch // 2 - 1, -1))
    near = list(range(n_patch // 2 - 1, -1, -1))
    first_terms, my_loads = first_products(order, loads, influence, share_rows, far[:1])
    rest = far[1:] + near
    more_terms = more_products(
        my_loads, influence, share_rows, rest, [BF16] * (len(rest) - 1) + [F32]
    )
    terms = list(first_terms) + list(more_terms)
    received = [swap(t, "patch", k) for k, t in zip(far + near[:-1], terms)]
    own = share_sum(terms[-1], received)

    position = block_position.reshape(n_hot * n_patch, 1, share_rows)
    top = n_patch // 2
    patch_bits = [1 << b for b in reversed(range((n_patch - 1).bit_length()))]
    chip_bits = [2 << b for b in reversed(range((n_hot // 2 - 1).bit_length()))]
    tie = lambda value, *after: lax.optimization_barrier((value, *after))[0]

    plane, pieces = {(0, 0): own}, {}

    def along(keys, axis, bits):
        for bit in bits:
            for j, k in list(keys):
                key = (j ^ bit, k) if axis == "hot" else (j, k ^ bit)
                plane[key] = swap(plane[j, k], axis, bit)
                keys = keys + [key]
        return keys

    def cores(keys):
        for j, k in keys:
            pieces[j, k] = plane[j, k]
            pieces[j + 1, k] = swap(plane[j, k], "hot", 1)
        return [(j + c, k) for j, k in keys for c in (0, 1)]

    def picked(keys, *before):
        return early_rows(block_pairs, position, keys, [pieces[key] for key in keys], before)

    head = cores([(0, 0)])
    along([(0, 0)], "patch", patch_bits[:1])
    near_keys = along([(0, 0)], "patch", patch_bits[1:])
    chip_keys = along([(0, 0)], "hot", chip_bits)
    for key in near_keys[1:] + chip_keys[1:]:
        plane[key] = tie(plane[key], plane[0, top])
    far_keys = along([(0, top)], "patch", patch_bits[1:])
    for j, _ in chip_keys[1:]:
        plane[j, n_patch - 1] = swap(plane[j, 0], "patch", n_patch - 1)
    early = picked(head + cores(near_keys[1:] + chip_keys[1:] + [(0, top)]))
    later = []
    for key in near_keys[1:] + far_keys[:-1]:
        later += along([key], "hot", chip_bits)[1:]
    middle = [key for key in later if key[1] < top]
    early = picked(cores(far_keys[1:] + middle), early)
    last = [key for key in plane if key not in pieces]
    for key in last:
        plane[key] = tie(plane[key], early)
    late = cores(last)
    return cross(
        block_pairs, position, weights, early, late, [pieces[key] for key in late], components
    )


def solution(mesh):
    placed = (
        P(None, "hot", "patch"),
        P("grp", None),
        P(),
        P("grp"),
        P(),
        P(("hot", "patch"), None),
    )
    return jax.shard_map(
        shards,
        mesh=mesh,
        in_specs=placed,
        out_specs=P(("grp", "hot", "patch"), None, None, None),
        check_vma=False,
    )
```

```python
import functools
import math

import jax
import jax.numpy as jnp
from jax import lax
from jax.experimental import pallas as pl
from jax.experimental.pallas import tpu as pltpu
from jax.sharding import PartitionSpec as P

BLK = 256
LANES = 128
F32 = jnp.float32
BF16 = jnp.bfloat16
VMEM_BYTES = 48 * 1024 * 1024
FIRST_VMEM_BYTES = 124 * 512 * 1024


def params(steps=1):
    return pltpu.CompilerParams(
        dimension_semantics=("arbitrary",) * steps, vmem_limit_bytes=VMEM_BYTES
    )


def cost(flops, bytes_accessed):
    return pl.CostEstimate(flops=flops, bytes_accessed=bytes_accessed, transcendentals=0)


def products(influence, my_loads, cuts, out_refs):
    components = influence.shape[1]
    columns = my_loads.shape[1]
    for (i, top, rows, kind), out_ref in zip(cuts, out_refs):
        for c in range(components):
            part = jnp.dot(influence[i, c, top : top + rows], my_loads, preferred_element_type=F32)
            out_ref[:, c * columns : (c + 1) * columns] = part.astype(kind)


def share_copies(influence_ref, held_ref, sems, which):
    rows = held_ref.shape[2]
    here = lax.axis_index("patch")
    return [
        pltpu.make_async_copy(
            influence_ref.at[:, pl.ds(pl.multiple_of((here ^ k) * rows, rows), rows), :],
            held_ref.at[i],
            sems.at[i],
        )
        for i, k in enumerate(which)
    ]


def first_kernel(which, cuts, order_ref, loads_ref, influence_ref, *refs):
    out_refs, (my_loads_ref, own_order, column_ref, table, pick_ref, held, sems) = refs[:-7], refs[-7:]
    columns = loads_ref.shape[1]
    half = loads_ref.shape[0] // 2
    order_copy = pltpu.make_async_copy(order_ref.at[lax.axis_index("patch")], own_order, sems.at[0])
    low_copy = pltpu.make_async_copy(
        loads_ref.at[pl.ds(0, half)], table.at[:, pl.ds(0, columns)], sems.at[1]
    )
    high_copy = pltpu.make_async_copy(
        loads_ref.at[pl.ds(half, half)], table.at[:, pl.ds(columns, columns)], sems.at[2]
    )
    copies = share_copies(influence_ref, held, sems.at[pl.ds(3, len(which))], which)
    order_copy.start()
    low_copy.start()
    high_copy.start()
    for copy in copies:
        copy.start()
    order_copy.wait()
    lane = lax.broadcasted_iota(jnp.int32, (LANES, LANES), 1)
    low_copy.wait()
    high_copy.wait()
    for g in range(own_order.shape[0] * LANES // 512):
        wanteds = []
        for h in range(512 // LANES):
            i = g * (512 // LANES) + h
            wanteds.append(jnp.transpose(jnp.broadcast_to(own_order[i : i + 1, :], (LANES, LANES))))
        wanted = jnp.concatenate(wanteds, axis=0)
        low = jnp.where(wanted >= half, wanted - half, wanted) - lax.broadcasted_iota(jnp.int32, wanted.shape, 1)
        pick = jnp.concatenate(
            [jnp.where(low == j * LANES, 1.0, 0.0).astype(BF16) for j in range(half // LANES)], axis=1
        )
        both = jnp.dot(pick, table[...], preferred_element_type=F32)
        my_loads_ref[g * 512 : (g + 1) * 512, :] = jnp.where(
            wanted >= half, both[:, columns:], both[:, :columns]
        ).astype(BF16)
    for copy in copies:
        copy.wait()
    products(held[...], my_loads_ref[...], cuts, out_refs)


def more_kernel(which, cuts, my_loads_ref, influence_ref, *refs):
    out_refs, (held, sems) = refs[:-2], refs[-2:]
    copies = share_copies(influence_ref, held, sems, which)
    for copy in copies:
        copy.start()
    for copy in copies:
        copy.wait()
    products(held[...], my_loads_ref[...], cuts, out_refs)


def vmem():
    return pl.BlockSpec(memory_space=pltpu.VMEM)


def hbm():
    return pl.BlockSpec(memory_space=pltpu.HBM)


def first_products(order, loads, influence, share_rows, which, cuts):
    components, _, patch_cols = influence.shape
    patches, columns = loads.shape
    cut_shapes = [jax.ShapeDtypeStruct((cut[2], components * columns), cut[3]) for cut in cuts]
    held = (len(which), components, share_rows, patch_cols)
    out = pl.pallas_call(
        functools.partial(first_kernel, which, cuts),
        out_shape=cut_shapes + [jax.ShapeDtypeStruct((patch_cols, columns), BF16)],
        in_specs=[hbm()] * 3,
        out_specs=[vmem()] * (len(cuts) + 1),
        scratch_shapes=[
            pltpu.VMEM(order.shape[1:], jnp.int32),
            pltpu.VMEM((patch_cols, columns), jnp.int32),
            pltpu.VMEM((patches // 2, 2 * columns), BF16),
            pltpu.VMEM((patch_cols, patches // 2), BF16),
            pltpu.VMEM(held, BF16),
            pltpu.SemaphoreType.DMA((3 + len(which),)),
        ],
        compiler_params=pltpu.CompilerParams(vmem_limit_bytes=FIRST_VMEM_BYTES),
        name="first_products",
    )(order, loads, influence)
    return out[:-1], out[-1]


def more_products(my_loads, influence, share_rows, which, cuts):
    components, _, patch_cols = influence.shape
    columns = my_loads.shape[1]
    cut_shapes = [jax.ShapeDtypeStruct((cut[2], components * columns), cut[3]) for cut in cuts]
    held = (len(which), components, share_rows, patch_cols)
    return pl.pallas_call(
        functools.partial(more_kernel, which, cuts),
        out_shape=cut_shapes,
        in_specs=[vmem(), hbm()],
        out_specs=[vmem()] * len(cuts),
        scratch_shapes=[pltpu.VMEM(held, BF16), pltpu.SemaphoreType.DMA((len(which),))],
        compiler_params=pltpu.CompilerParams(vmem_limit_bytes=VMEM_BYTES),
        cost_estimate=cost(2 * columns * math.prod(held), 2 * math.prod(held)),
        name="more_products",
    )(my_loads, influence)


def sum_kernel(kind, own_ref, *refs):
    total = own_ref[...]
    for ref in refs[:-1]:
        total = total + ref[...].astype(F32)
    refs[-1][...] = total.astype(kind)


def total_kernel(near, own_ref, *refs):
    out_ref, half = refs[-1], refs[-2].shape[0]
    for top, terms in ((0, refs[near:-2]), (half, refs[-2:-1])):
        rows = slice(top, top + half)
        total = own_ref[rows, :]
        for ref in refs[:near]:
            total = total + ref[rows, :].astype(F32)
        for ref in terms:
            total = total + ref[...].astype(F32)
        out_ref[rows, :] = total.astype(BF16)


def summed(kernel, own, others, name):
    return pl.pallas_call(
        kernel,
        out_shape=jax.ShapeDtypeStruct(own.shape, BF16),
        in_specs=[vmem()] * (1 + len(others)),
        out_specs=vmem(),
        compiler_params=pltpu.CompilerParams(vmem_limit_bytes=VMEM_BYTES),
        name=name,
    )(own, *others)


def pick_rows(position_ref, key, block):
    n_patch = lax.axis_size("patch")
    place = (lax.axis_index("hot") ^ key[0]) * n_patch + (lax.axis_index("patch") ^ key[1])
    rows = position_ref.shape[2]
    offset = position_ref[place] - block * BLK
    return jnp.where(offset == lax.broadcasted_iota(jnp.int32, (BLK, rows), 0), 1.0, 0.0).astype(BF16)


def pick_group(position_ref, groups, block):
    picks = [pick_rows(position_ref, key, block) for keys in groups for key in keys]
    return jnp.concatenate(picks, axis=1)


def join_kernel(*refs):
    rows = refs[0].shape[0]
    for i, ref in enumerate(refs[:-1]):
        refs[-1][i * rows : (i + 1) * rows, :] = ref[...]


def join(pieces):
    rows, width = pieces[0].shape
    return pl.pallas_call(
        join_kernel,
        out_shape=jax.ShapeDtypeStruct((len(pieces) * rows, width), BF16),
        in_specs=[vmem()] * len(pieces),
        out_specs=vmem(),
        compiler_params=pltpu.CompilerParams(vmem_limit_bytes=VMEM_BYTES),
        name="join",
    )(*pieces)


def early_kernel(groups, pairs_ref, position_ref, *refs):
    count = len(groups)
    pieces, befores, (out_ref, joined_ref) = refs[:count], refs[count:-2], refs[-2:]
    rows = pieces[0].shape[0]
    for i, piece in enumerate(pieces):
        joined_ref[i * rows : (i + 1) * rows, :] = piece[...]
    for s in range(out_ref.shape[0]):
        pick = pick_group(position_ref, groups, pairs_ref[s // 2, s % 2])
        total = jnp.dot(pick, joined_ref[...], preferred_element_type=F32)
        out_ref[s] = total + befores[0][s] if befores else total


def early_rows(pairs, position, groups, pieces, before=()):
    count = pairs.shape[0] * 2
    rows, width = pieces[0].shape
    flops = 2 * count * BLK * rows * width * len(groups)
    return pl.pallas_call(
        functools.partial(early_kernel, groups),
        out_shape=jax.ShapeDtypeStruct((count, BLK, width), F32),
        in_specs=[pl.BlockSpec(memory_space=pltpu.SMEM)] + [vmem()] * (1 + len(pieces) + len(before)),
        out_specs=vmem(),
        scratch_shapes=[pltpu.VMEM((len(groups) * rows, width), BF16)],
        compiler_params=pltpu.CompilerParams(vmem_limit_bytes=VMEM_BYTES),
        cost_estimate=cost(2 * flops, 8 * count * BLK * width),
        name="early_rows",
    )(pairs, position, *pieces, *before)


def cross_kernel(components, groups, pairs_ref, position_ref, weights_ref, early_ref, *refs):
    pieces, (out_ref, left_ref, right_ref, joined_ref) = refs[:-4], refs[-4:]
    q = pl.program_id(0)
    columns = weights_ref.shape[1]
    rows = pieces[0].shape[0]

    @pl.when(q == 0)
    def _():
        for i, piece in enumerate(pieces):
            joined_ref[i * rows : (i + 1) * rows, :] = piece[...]

    for side, rows_ref in ((0, left_ref), (1, right_ref)):
        pick = pick_group(position_ref, groups, pairs_ref[q, side])
        total = jnp.dot(pick, joined_ref[...], preferred_element_type=F32) + early_ref[2 * q + side]
        for c in range(components):
            rows_ref[pl.ds(c, BLK, stride=components), :] = total[:, c * columns : (c + 1) * columns]
    scaled = (left_ref[...] * weights_ref[...]).astype(BF16)
    right = right_ref[...]
    lane = lax.broadcasted_iota(jnp.int32, right.shape, 1)
    turned = pltpu.roll(right, columns // 2, 1)
    turned = jnp.where(lane < columns // 2, -turned, turned)
    for part, other in ((0, right), (1, turned)):
        out_ref[0, part] = lax.dot_general(
            scaled, other.astype(BF16), (((1,), (1,)), ((), ())), preferred_element_type=F32
        ).astype(BF16)


def cross(pairs, position, weights, early, groups, pieces, components):
    count = pairs.shape[0]
    columns = weights.shape[1]
    rows = BLK * components
    return pl.pallas_call(
        functools.partial(cross_kernel, components, groups),
        out_shape=jax.ShapeDtypeStruct((count, 2, rows, rows), BF16),
        grid=(count,),
        in_specs=[pl.BlockSpec(memory_space=pltpu.SMEM)] + [vmem()] * (3 + len(pieces)),
        out_specs=pl.BlockSpec((1, 2, rows, rows), lambda i: (i, 0, 0, 0)),
        scratch_shapes=[
            pltpu.VMEM((rows, columns), F32),
            pltpu.VMEM((rows, columns), F32),
            pltpu.VMEM((len(pieces) * pieces[0].shape[0], components * columns), BF16),
        ],
        compiler_params=params(),
        name="cross",
    )(pairs, position, weights, early, *pieces)


def shards(influence, loads, patch_order, spectral_weights, block_position, block_pairs):
    components, hot_rows, patch_cols = influence.shape
    n_patch, n_hot = lax.axis_size("patch"), lax.axis_size("hot")
    share_rows = hot_rows // n_patch
    weights = jnp.concatenate([spectral_weights, spectral_weights])[None, :]
    order = patch_order.reshape(n_patch, patch_cols // LANES, LANES)

    def swap(array, axis, k):
        size = lax.axis_size(axis)
        return lax.ppermute(array, axis, [(i, i ^ k) for i in range(size)])

    far = list(range(n_patch - 1, n_patch // 2 - 1, -1))
    near = list(range(n_patch // 2 - 1, -1, -1))
    tie = lambda value, *after: lax.optimization_barrier((value, *after))[0]

    top = n_patch // 2
    half = share_rows // 2

    def halves(i, kind):
        return [(i, 0, half, BF16), (i, half, half, kind)]

    first_terms, my_loads = first_products(
        order, loads, influence, share_rows, far[:1], halves(0, BF16 if n_patch > 2 else F32)
    )
    rest = far[1:] + near
    cuts = []
    for i, k in enumerate(rest):
        if k >= top:
            cuts += halves(i, BF16 if k > top else F32)
        else:
            cuts.append((i, 0, share_rows, BF16 if k else F32))
    terms = list(first_terms) + list(more_products(my_loads, influence, share_rows, rest, cuts))
    straight = dict(zip(far, terms[0 : 2 * len(far) : 2]))
    lower = dict(zip(far, terms[1 : 2 * len(far) : 2]))
    carried = [swap(lower[k], "patch", k ^ top) for k in far if k != top]
    from_far = [swap(straight[k], "patch", k) for k in far]
    from_near = [
        swap(tie(term, *carried), "patch", k) for k, term in zip(near[:-1], terms[2 * len(far) :])
    ]
    passed = swap(
        summed(functools.partial(sum_kernel, BF16), tie(lower[top], *from_far[:-1]), carried, "pass_sum"), "patch", top
    )
    own = summed(
        functools.partial(total_kernel, len(from_near)), terms[-1], from_near + from_far + [passed], "share_sum"
    )

    position = block_position.reshape(n_hot * n_patch, 1, share_rows)
    patch_bits = [1 << b for b in reversed(range((n_patch - 1).bit_length()))]
    chip_bits = [2 << b for b in reversed(range((n_hot // 2 - 1).bit_length()))]

    plane = {(0, 0): own}

    def along(keys, axis, bits):
        for bit in bits:
            for j, k in list(keys):
                key = (j ^ bit, k) if axis == "hot" else (j, k ^ bit)
                plane[key] = swap(plane[j, k], axis, bit)
                keys = keys + [key]
        return keys

    def cores(keys, *after):
        mine = join([plane[key] for key in keys])
        other = swap(tie(mine, *after), "hot", 1)
        return [keys, [(j + 1, k) for j, k in keys]], [mine, other]

    def picked(group, *before):
        return early_rows(block_pairs, position, *group, before)

    along([(0, 0)], "patch", patch_bits[:1])
    near_keys = along([(0, 0)], "patch", patch_bits[1:])
    chip_keys = along([(0, 0)], "hot", chip_bits)
    head = cores([(0, 0)])
    early = picked(head)
    for key in near_keys[1:] + chip_keys[1:]:
        plane[key] = tie(plane[key], plane[0, top])
    far_keys = along([(0, top)], "patch", patch_bits[1:])
    for j, _ in chip_keys[1:]:
        start = tie(plane[j, 0], plane[0, top])
        plane[j, n_patch - 1] = swap(start, "patch", n_patch - 1)
    middle = []
    for key in near_keys[1:]:
        middle += along([key], "hot", chip_bits)[1:]
    for key in far_keys[:-1]:
        along([key], "hot", chip_bits)
    early = picked(cores(near_keys[1:] + chip_keys[1:] + [(0, top)], head[1][1]), early)
    before = early
    early = picked(cores(middle + far_keys[1:]), early)
    done = chip_keys + near_keys + [(0, top)] + middle + far_keys
    last = [key for key in plane if key not in done]
    for key in last:
        plane[key] = tie(plane[key], before)
    groups, pieces = cores(last)
    return cross(block_pairs, position, weights, early, groups, pieces, components)


def solution(mesh):
    placed = (
        P(None, "hot", "patch"),
        P("grp", None),
        P(),
        P("grp"),
        P(),
        P(("hot", "patch"), None),
    )
    return jax.shard_map(
        shards,
        mesh=mesh,
        in_specs=placed,
        out_specs=P(("grp", "hot", "patch"), None, None, None),
        check_vma=False,
    )
```

```python
import functools
import math

import jax
import jax.numpy as jnp
from jax import lax
from jax.experimental import pallas as pl
from jax.experimental.pallas import tpu as pltpu
from jax.sharding import PartitionSpec as P

BLK = 256
LANES = 128
F32 = jnp.float32
BF16 = jnp.bfloat16
VMEM_BYTES = 48 * 1024 * 1024
FIRST_VMEM_BYTES = 124 * 512 * 1024


def params(steps=1):
    return pltpu.CompilerParams(
        dimension_semantics=("arbitrary",) * steps, vmem_limit_bytes=VMEM_BYTES
    )


def cost(flops, bytes_accessed):
    return pl.CostEstimate(flops=flops, bytes_accessed=bytes_accessed, transcendentals=0)


def products(influence, my_loads, cuts, out_refs):
    components = influence.shape[1]
    columns = my_loads.shape[1]
    for (i, top, rows, kind), out_ref in zip(cuts, out_refs):
        for c in range(components):
            part = jnp.dot(influence[i, c, top : top + rows], my_loads, preferred_element_type=F32)
            out_ref[:, c * columns : (c + 1) * columns] = part.astype(kind)


def share_copies(influence_ref, held_ref, sems, which):
    rows = held_ref.shape[2]
    here = lax.axis_index("patch")
    return [
        pltpu.make_async_copy(
            influence_ref.at[:, pl.ds(pl.multiple_of((here ^ k) * rows, rows), rows), :],
            held_ref.at[i],
            sems.at[i],
        )
        for i, k in enumerate(which)
    ]


def first_kernel(which, cuts, order_ref, loads_ref, influence_ref, *refs):
    out_refs, (my_loads_ref, own_order, column_ref, table, pick_ref, held, sems) = refs[:-7], refs[-7:]
    columns = loads_ref.shape[1]
    half = loads_ref.shape[0] // 2
    order_copy = pltpu.make_async_copy(order_ref.at[lax.axis_index("patch")], own_order, sems.at[0])
    low_copy = pltpu.make_async_copy(
        loads_ref.at[pl.ds(0, half)], table.at[:, pl.ds(0, columns)], sems.at[1]
    )
    high_copy = pltpu.make_async_copy(
        loads_ref.at[pl.ds(half, half)], table.at[:, pl.ds(columns, columns)], sems.at[2]
    )
    copies = share_copies(influence_ref, held, sems.at[pl.ds(3, len(which))], which)
    order_copy.start()
    low_copy.start()
    high_copy.start()
    for copy in copies:
        copy.start()
    order_copy.wait()
    lane = lax.broadcasted_iota(jnp.int32, (LANES, LANES), 1)
    low_copy.wait()
    high_copy.wait()
    for g in range(own_order.shape[0] * LANES // 512):
        wanteds = []
        for h in range(512 // LANES):
            i = g * (512 // LANES) + h
            wanteds.append(jnp.transpose(jnp.broadcast_to(own_order[i : i + 1, :], (LANES, LANES))))
        wanted = jnp.concatenate(wanteds, axis=0)
        low = jnp.where(wanted >= half, wanted - half, wanted) - lax.broadcasted_iota(jnp.int32, wanted.shape, 1)
        pick = jnp.concatenate(
            [jnp.where(low == j * LANES, 1.0, 0.0).astype(BF16) for j in range(half // LANES)], axis=1
        )
        both = jnp.dot(pick, table[...], preferred_element_type=F32)
        my_loads_ref[g * 512 : (g + 1) * 512, :] = jnp.where(
            wanted >= half, both[:, columns:], both[:, :columns]
        ).astype(BF16)
    for copy in copies:
        copy.wait()
    products(held[...], my_loads_ref[...], cuts, out_refs)


def more_kernel(which, cuts, my_loads_ref, influence_ref, *refs):
    out_refs, (held, sems) = refs[:-2], refs[-2:]
    copies = share_copies(influence_ref, held, sems, which)
    for copy in copies:
        copy.start()
    for copy in copies:
        copy.wait()
    products(held[...], my_loads_ref[...], cuts, out_refs)


def vmem():
    return pl.BlockSpec(memory_space=pltpu.VMEM)


def hbm():
    return pl.BlockSpec(memory_space=pltpu.HBM)


def first_products(order, loads, influence, share_rows, which, cuts):
    components, _, patch_cols = influence.shape
    patches, columns = loads.shape
    cut_shapes = [jax.ShapeDtypeStruct((cut[2], components * columns), cut[3]) for cut in cuts]
    held = (len(which), components, share_rows, patch_cols)
    out = pl.pallas_call(
        functools.partial(first_kernel, which, cuts),
        out_shape=cut_shapes + [jax.ShapeDtypeStruct((patch_cols, columns), BF16)],
        in_specs=[hbm()] * 3,
        out_specs=[vmem()] * (len(cuts) + 1),
        scratch_shapes=[
            pltpu.VMEM(order.shape[1:], jnp.int32),
            pltpu.VMEM((patch_cols, columns), jnp.int32),
            pltpu.VMEM((patches // 2, 2 * columns), BF16),
            pltpu.VMEM((patch_cols, patches // 2), BF16),
            pltpu.VMEM(held, BF16),
            pltpu.SemaphoreType.DMA((3 + len(which),)),
        ],
        compiler_params=pltpu.CompilerParams(vmem_limit_bytes=FIRST_VMEM_BYTES),
        name="first_products",
    )(order, loads, influence)
    return out[:-1], out[-1]


def more_products(my_loads, influence, share_rows, which, cuts):
    components, _, patch_cols = influence.shape
    columns = my_loads.shape[1]
    cut_shapes = [jax.ShapeDtypeStruct((cut[2], components * columns), cut[3]) for cut in cuts]
    held = (len(which), components, share_rows, patch_cols)
    return pl.pallas_call(
        functools.partial(more_kernel, which, cuts),
        out_shape=cut_shapes,
        in_specs=[vmem(), hbm()],
        out_specs=[vmem()] * len(cuts),
        scratch_shapes=[pltpu.VMEM(held, BF16), pltpu.SemaphoreType.DMA((len(which),))],
        compiler_params=pltpu.CompilerParams(vmem_limit_bytes=VMEM_BYTES),
        cost_estimate=cost(2 * columns * math.prod(held), 2 * math.prod(held)),
        name="more_products",
    )(my_loads, influence)


def sum_kernel(kind, own_ref, *refs):
    total = own_ref[...]
    for ref in refs[:-1]:
        total = total + ref[...].astype(F32)
    refs[-1][...] = total.astype(kind)


def total_kernel(near, own_ref, *refs):
    out_ref, half = refs[-1], refs[-2].shape[0]
    for top, terms in ((0, refs[near:-2]), (half, refs[-2:-1])):
        rows = slice(top, top + half)
        total = own_ref[rows, :]
        for ref in refs[:near]:
            total = total + ref[rows, :].astype(F32)
        for ref in terms:
            total = total + ref[...].astype(F32)
        out_ref[rows, :] = total.astype(BF16)


def summed(kernel, own, others, name):
    return pl.pallas_call(
        kernel,
        out_shape=jax.ShapeDtypeStruct(own.shape, BF16),
        in_specs=[vmem()] * (1 + len(others)),
        out_specs=vmem(),
        compiler_params=pltpu.CompilerParams(vmem_limit_bytes=VMEM_BYTES),
        name=name,
    )(own, *others)


def pick_rows(position_ref, key, block):
    n_patch = lax.axis_size("patch")
    place = (lax.axis_index("hot") ^ key[0]) * n_patch + (lax.axis_index("patch") ^ key[1])
    rows = position_ref.shape[2]
    offset = position_ref[place] - block * BLK
    return jnp.where(offset == lax.broadcasted_iota(jnp.int32, (BLK, rows), 0), 1.0, 0.0).astype(BF16)


def pick_group(position_ref, groups, block):
    picks = [pick_rows(position_ref, key, block) for keys in groups for key in keys]
    return jnp.concatenate(picks, axis=1)


def join_kernel(*refs):
    rows = refs[0].shape[0]
    for i, ref in enumerate(refs[:-1]):
        refs[-1][i * rows : (i + 1) * rows, :] = ref[...]


def join(pieces):
    rows, width = pieces[0].shape
    return pl.pallas_call(
        join_kernel,
        out_shape=jax.ShapeDtypeStruct((len(pieces) * rows, width), BF16),
        in_specs=[vmem()] * len(pieces),
        out_specs=vmem(),
        compiler_params=pltpu.CompilerParams(vmem_limit_bytes=VMEM_BYTES),
        name="join",
    )(*pieces)


def early_kernel(groups, pairs_ref, position_ref, *refs):
    count = len(groups)
    pieces, befores, (out_ref, joined_ref) = refs[:count], refs[count:-2], refs[-2:]
    rows = pieces[0].shape[0]
    for i, piece in enumerate(pieces):
        joined_ref[i * rows : (i + 1) * rows, :] = piece[...]
    for s in range(out_ref.shape[0]):
        pick = pick_group(position_ref, groups, pairs_ref[s // 2, s % 2])
        total = jnp.dot(pick, joined_ref[...], preferred_element_type=F32)
        out_ref[s] = total + befores[0][s] if befores else total


def early_rows(pairs, position, groups, pieces, before=()):
    count = pairs.shape[0] * 2
    rows, width = pieces[0].shape
    flops = 2 * count * BLK * rows * width * len(groups)
    return pl.pallas_call(
        functools.partial(early_kernel, groups),
        out_shape=jax.ShapeDtypeStruct((count, BLK, width), F32),
        in_specs=[pl.BlockSpec(memory_space=pltpu.SMEM)] + [vmem()] * (1 + len(pieces) + len(before)),
        out_specs=vmem(),
        scratch_shapes=[pltpu.VMEM((len(groups) * rows, width), BF16)],
        compiler_params=pltpu.CompilerParams(vmem_limit_bytes=VMEM_BYTES),
        cost_estimate=cost(2 * flops, 8 * count * BLK * width),
        name="early_rows",
    )(pairs, position, *pieces, *before)


def cross_kernel(components, groups, pairs_ref, position_ref, weights_ref, early_ref, *refs):
    pieces, (out_ref, left_ref, right_ref, joined_ref, done_ref, sems) = refs[:-6], refs[-6:]
    columns = weights_ref.shape[1]
    rows = pieces[0].shape[0]
    for i, piece in enumerate(pieces):
        joined_ref[i * rows : (i + 1) * rows, :] = piece[...]
    copies = []
    for q in range(out_ref.shape[0]):
        for side, rows_ref in ((0, left_ref), (1, right_ref)):
            pick = pick_group(position_ref, groups, pairs_ref[q, side])
            total = jnp.dot(pick, joined_ref[...], preferred_element_type=F32) + early_ref[2 * q + side]
            for c in range(components):
                rows_ref[q, pl.ds(c, BLK, stride=components), :] = total[:, c * columns : (c + 1) * columns]
        scaled = (left_ref[q] * weights_ref[...]).astype(BF16)
        right = right_ref[q]
        lane = lax.broadcasted_iota(jnp.int32, right.shape, 1)
        turned = pltpu.roll(right, columns // 2, 1)
        turned = jnp.where(lane < columns // 2, -turned, turned)
        for part, other in ((0, right), (1, turned)):
            other = other.astype(BF16)
            for top in range(0, scaled.shape[0], BLK):
                done_ref[q, part, top : top + BLK, :] = lax.dot_general(
                    scaled[top : top + BLK], other, (((1,), (1,)), ((), ())), preferred_element_type=F32
                ).astype(BF16)
            copy = pltpu.make_async_copy(done_ref.at[q, part], out_ref.at[q, part], sems.at[q, part])
            copy.start()
            copies.append(copy)
    for copy in copies:
        copy.wait()


def cross(pairs, position, weights, early, groups, pieces, components):
    count = pairs.shape[0]
    columns = weights.shape[1]
    rows = BLK * components
    out = jax.ShapeDtypeStruct((count, 2, rows, rows), BF16)
    return pl.pallas_call(
        functools.partial(cross_kernel, components, groups),
        out_shape=out,
        in_specs=[pl.BlockSpec(memory_space=pltpu.SMEM)] + [vmem()] * (3 + len(pieces)),
        out_specs=hbm(),
        scratch_shapes=[
            pltpu.VMEM((count, rows, columns), F32),
            pltpu.VMEM((count, rows, columns), F32),
            pltpu.VMEM((len(pieces) * pieces[0].shape[0], components * columns), BF16),
            pltpu.VMEM(out.shape, BF16),
            pltpu.SemaphoreType.DMA((count, 2)),
        ],
        compiler_params=pltpu.CompilerParams(vmem_limit_bytes=VMEM_BYTES),
        name="cross",
    )(pairs, position, weights, early, *pieces)


def shards(influence, loads, patch_order, spectral_weights, block_position, block_pairs):
    components, hot_rows, patch_cols = influence.shape
    n_patch, n_hot = lax.axis_size("patch"), lax.axis_size("hot")
    share_rows = hot_rows // n_patch
    weights = jnp.concatenate([spectral_weights, spectral_weights])[None, :]
    order = patch_order.reshape(n_patch, patch_cols // LANES, LANES)

    def swap(array, axis, k):
        size = lax.axis_size(axis)
        return lax.ppermute(array, axis, [(i, i ^ k) for i in range(size)])

    far = list(range(n_patch - 1, n_patch // 2 - 1, -1))
    near = list(range(n_patch // 2 - 1, -1, -1))
    tie = lambda value, *after: lax.optimization_barrier((value, *after))[0]

    top = n_patch // 2
    half = share_rows // 2

    def halves(i, kind):
        return [(i, 0, half, BF16), (i, half, half, kind)]

    first_terms, my_loads = first_products(
        order, loads, influence, share_rows, far[:1], halves(0, BF16 if n_patch > 2 else F32)
    )
    rest = far[1:] + near
    cuts = []
    for i, k in enumerate(rest):
        if k >= top:
            cuts += halves(i, BF16 if k > top else F32)
        else:
            cuts.append((i, 0, share_rows, BF16 if k else F32))
    terms = list(first_terms) + list(more_products(my_loads, influence, share_rows, rest, cuts))
    straight = dict(zip(far, terms[0 : 2 * len(far) : 2]))
    lower = dict(zip(far, terms[1 : 2 * len(far) : 2]))
    carried = [swap(lower[k], "patch", k ^ top) for k in far if k != top]
    from_far = [swap(straight[k], "patch", k) for k in far]
    from_near = [
        swap(tie(term, *carried), "patch", k) for k, term in zip(near[:-1], terms[2 * len(far) :])
    ]
    passed = swap(
        summed(functools.partial(sum_kernel, BF16), tie(lower[top], *from_far[:-1]), carried, "pass_sum"), "patch", top
    )
    own = summed(
        functools.partial(total_kernel, len(from_near)), terms[-1], from_near + from_far + [passed], "share_sum"
    )

    position = block_position.reshape(n_hot * n_patch, 1, share_rows)
    patch_bits = [1 << b for b in reversed(range((n_patch - 1).bit_length()))]
    chip_bits = [2 << b for b in reversed(range((n_hot // 2 - 1).bit_length()))]

    plane = {(0, 0): own}

    def along(keys, axis, bits):
        for bit in bits:
            for j, k in list(keys):
                key = (j ^ bit, k) if axis == "hot" else (j, k ^ bit)
                plane[key] = swap(plane[j, k], axis, bit)
                keys = keys + [key]
        return keys

    def cores(keys, *after):
        mine = join([plane[key] for key in keys])
        other = swap(tie(mine, *after), "hot", 1)
        return [keys, [(j + 1, k) for j, k in keys]], [mine, other]

    def picked(group, *before):
        return early_rows(block_pairs, position, *group, before)

    along([(0, 0)], "patch", patch_bits[:1])
    near_keys = along([(0, 0)], "patch", patch_bits[1:])
    chip_keys = along([(0, 0)], "hot", chip_bits)
    head = cores([(0, 0)])
    early = picked(head)
    for key in near_keys[1:] + chip_keys[1:]:
        plane[key] = tie(plane[key], plane[0, top])
    far_keys = along([(0, top)], "patch", patch_bits[1:])
    for j, _ in chip_keys[1:]:
        start = tie(plane[j, 0], plane[0, top])
        plane[j, n_patch - 1] = swap(start, "patch", n_patch - 1)
    middle = []
    for key in near_keys[1:]:
        middle += along([key], "hot", chip_bits)[1:]
    for key in far_keys[:-1]:
        along([key], "hot", chip_bits)
    early = picked(cores(near_keys[1:] + chip_keys[1:] + [(0, top)], head[1][1]), early)
    before = early
    early = picked(cores(middle + far_keys[1:]), early)
    done = chip_keys + near_keys + [(0, top)] + middle + far_keys
    last = [key for key in plane if key not in done]
    for key in last:
        plane[key] = tie(plane[key], before)
    groups, pieces = cores(last)
    return cross(block_pairs, position, weights, early, groups, pieces, components)


def solution(mesh):
    placed = (
        P(None, "hot", "patch"),
        P("grp", None),
        P(),
        P("grp"),
        P(),
        P(("hot", "patch"), None),
    )
    return jax.shard_map(
        shards,
        mesh=mesh,
        in_specs=placed,
        out_specs=P(("grp", "hot", "patch"), None, None, None),
        check_vma=False,
    )
```

```python
import functools
import math

import jax
import jax.numpy as jnp
from jax import lax
from jax.experimental import pallas as pl
from jax.experimental.pallas import tpu as pltpu
from jax.sharding import PartitionSpec as P

BLK = 256
LANES = 128
F32 = jnp.float32
BF16 = jnp.bfloat16
VMEM_BYTES = 48 * 1024 * 1024
FIRST_VMEM_BYTES = 124 * 512 * 1024


def params(steps=1):
    return pltpu.CompilerParams(
        dimension_semantics=("arbitrary",) * steps, vmem_limit_bytes=VMEM_BYTES
    )


def cost(flops, bytes_accessed):
    return pl.CostEstimate(flops=flops, bytes_accessed=bytes_accessed, transcendentals=0)


def products(influence, my_loads, cuts, out_refs):
    components = influence.shape[1]
    columns = my_loads.shape[1]
    for (i, top, rows, kind), out_ref in zip(cuts, out_refs):
        for c in range(components):
            part = jnp.dot(influence[i, c, top : top + rows], my_loads, preferred_element_type=F32)
            out_ref[:, c * columns : (c + 1) * columns] = part.astype(kind)


def share_copies(influence_ref, held_ref, sems, which):
    rows = held_ref.shape[2]
    here = lax.axis_index("patch")
    return [
        pltpu.make_async_copy(
            influence_ref.at[:, pl.ds(pl.multiple_of((here ^ k) * rows, rows), rows), :],
            held_ref.at[i],
            sems.at[i],
        )
        for i, k in enumerate(which)
    ]


def first_kernel(which, cuts, order_ref, loads_ref, influence_ref, *refs):
    out_refs, (my_loads_ref, own_order, column_ref, table, pick_ref, held, sems) = refs[:-7], refs[-7:]
    columns = loads_ref.shape[1]
    half = loads_ref.shape[0] // 2
    order_copy = pltpu.make_async_copy(order_ref.at[lax.axis_index("patch")], own_order, sems.at[0])
    low_copy = pltpu.make_async_copy(
        loads_ref.at[pl.ds(0, half)], table.at[:, pl.ds(0, columns)], sems.at[1]
    )
    high_copy = pltpu.make_async_copy(
        loads_ref.at[pl.ds(half, half)], table.at[:, pl.ds(columns, columns)], sems.at[2]
    )
    copies = share_copies(influence_ref, held, sems.at[pl.ds(3, len(which))], which)
    order_copy.start()
    low_copy.start()
    high_copy.start()
    for copy in copies:
        copy.start()
    order_copy.wait()
    lane = lax.broadcasted_iota(jnp.int32, (LANES, LANES), 1)
    low_copy.wait()
    high_copy.wait()
    for g in range(own_order.shape[0] * LANES // 512):
        wanteds = []
        for h in range(512 // LANES):
            i = g * (512 // LANES) + h
            wanteds.append(jnp.transpose(jnp.broadcast_to(own_order[i : i + 1, :], (LANES, LANES))))
        wanted = jnp.concatenate(wanteds, axis=0)
        low = jnp.where(wanted >= half, wanted - half, wanted) - lax.broadcasted_iota(jnp.int32, wanted.shape, 1)
        pick = jnp.concatenate(
            [jnp.where(low == j * LANES, 1.0, 0.0).astype(BF16) for j in range(half // LANES)], axis=1
        )
        both = jnp.dot(pick, table[...], preferred_element_type=F32)
        my_loads_ref[g * 512 : (g + 1) * 512, :] = jnp.where(
            wanted >= half, both[:, columns:], both[:, :columns]
        ).astype(BF16)
    for copy in copies:
        copy.wait()
    products(held[...], my_loads_ref[...], cuts, out_refs)


def more_kernel(which, cuts, my_loads_ref, influence_ref, *refs):
    out_refs, (held, sems) = refs[:-2], refs[-2:]
    copies = share_copies(influence_ref, held, sems, which)
    for copy in copies:
        copy.start()
    for copy in copies:
        copy.wait()
    products(held[...], my_loads_ref[...], cuts, out_refs)


def vmem():
    return pl.BlockSpec(memory_space=pltpu.VMEM)


def hbm():
    return pl.BlockSpec(memory_space=pltpu.HBM)


def first_products(order, loads, influence, share_rows, which, cuts):
    components, _, patch_cols = influence.shape
    patches, columns = loads.shape
    cut_shapes = [jax.ShapeDtypeStruct((cut[2], components * columns), cut[3]) for cut in cuts]
    held = (len(which), components, share_rows, patch_cols)
    out = pl.pallas_call(
        functools.partial(first_kernel, which, cuts),
        out_shape=cut_shapes + [jax.ShapeDtypeStruct((patch_cols, columns), BF16)],
        in_specs=[hbm()] * 3,
        out_specs=[vmem()] * (len(cuts) + 1),
        scratch_shapes=[
            pltpu.VMEM(order.shape[1:], jnp.int32),
            pltpu.VMEM((patch_cols, columns), jnp.int32),
            pltpu.VMEM((patches // 2, 2 * columns), BF16),
            pltpu.VMEM((patch_cols, patches // 2), BF16),
            pltpu.VMEM(held, BF16),
            pltpu.SemaphoreType.DMA((3 + len(which),)),
        ],
        compiler_params=pltpu.CompilerParams(vmem_limit_bytes=FIRST_VMEM_BYTES),
        name="first_products",
    )(order, loads, influence)
    return out[:-1], out[-1]


def more_products(my_loads, influence, share_rows, which, cuts):
    components, _, patch_cols = influence.shape
    columns = my_loads.shape[1]
    cut_shapes = [jax.ShapeDtypeStruct((cut[2], components * columns), cut[3]) for cut in cuts]
    held = (len(which), components, share_rows, patch_cols)
    return pl.pallas_call(
        functools.partial(more_kernel, which, cuts),
        out_shape=cut_shapes,
        in_specs=[vmem(), hbm()],
        out_specs=[vmem()] * len(cuts),
        scratch_shapes=[pltpu.VMEM(held, BF16), pltpu.SemaphoreType.DMA((len(which),))],
        compiler_params=pltpu.CompilerParams(vmem_limit_bytes=VMEM_BYTES),
        cost_estimate=cost(2 * columns * math.prod(held), 2 * math.prod(held)),
        name="more_products",
    )(my_loads, influence)


def sum_kernel(kind, own_ref, *refs):
    total = own_ref[...]
    for ref in refs[:-1]:
        total = total + ref[...].astype(F32)
    refs[-1][...] = total.astype(kind)


def total_kernel(near, own_ref, *refs):
    out_ref = refs[-1]
    rest = refs[-2].shape[0]
    half = out_ref.shape[0] - rest
    for top, held, terms in ((0, half, refs[near:-2]), (half, rest, refs[-2:-1])):
        rows = slice(top, top + held)
        total = own_ref[rows, :]
        for ref in refs[:near]:
            total = total + ref[rows, :].astype(F32)
        for ref in terms:
            total = total + ref[...].astype(F32)
        out_ref[rows, :] = total.astype(BF16)


def summed(kernel, own, others, name):
    return pl.pallas_call(
        kernel,
        out_shape=jax.ShapeDtypeStruct(own.shape, BF16),
        in_specs=[vmem()] * (1 + len(others)),
        out_specs=vmem(),
        compiler_params=pltpu.CompilerParams(vmem_limit_bytes=VMEM_BYTES),
        name=name,
    )(own, *others)


def pick_rows(position_ref, key, block):
    n_patch = lax.axis_size("patch")
    place = (lax.axis_index("hot") ^ key[0]) * n_patch + (lax.axis_index("patch") ^ key[1])
    rows = position_ref.shape[2]
    offset = position_ref[place] - block * BLK
    return jnp.where(offset == lax.broadcasted_iota(jnp.int32, (BLK, rows), 0), 1.0, 0.0).astype(BF16)


def pick_group(position_ref, groups, block):
    picks = [pick_rows(position_ref, key, block) for keys in groups for key in keys]
    return jnp.concatenate(picks, axis=1)


def join_kernel(*refs):
    rows = refs[0].shape[0]
    for i, ref in enumerate(refs[:-1]):
        refs[-1][i * rows : (i + 1) * rows, :] = ref[...]


def join(pieces):
    rows, width = pieces[0].shape
    return pl.pallas_call(
        join_kernel,
        out_shape=jax.ShapeDtypeStruct((len(pieces) * rows, width), BF16),
        in_specs=[vmem()] * len(pieces),
        out_specs=vmem(),
        compiler_params=pltpu.CompilerParams(vmem_limit_bytes=VMEM_BYTES),
        name="join",
    )(*pieces)


def early_kernel(groups, pairs_ref, position_ref, *refs):
    count = len(groups)
    pieces, befores, (out_ref, joined_ref) = refs[:count], refs[count:-2], refs[-2:]
    rows = pieces[0].shape[0]
    for i, piece in enumerate(pieces):
        joined_ref[i * rows : (i + 1) * rows, :] = piece[...]
    for s in range(out_ref.shape[0]):
        pick = pick_group(position_ref, groups, pairs_ref[s // 2, s % 2])
        total = jnp.dot(pick, joined_ref[...], preferred_element_type=F32)
        out_ref[s] = total + befores[0][s] if befores else total


def early_rows(pairs, position, groups, pieces, before=()):
    count = pairs.shape[0] * 2
    rows, width = pieces[0].shape
    flops = 2 * count * BLK * rows * width * len(groups)
    return pl.pallas_call(
        functools.partial(early_kernel, groups),
        out_shape=jax.ShapeDtypeStruct((count, BLK, width), F32),
        in_specs=[pl.BlockSpec(memory_space=pltpu.SMEM)] + [vmem()] * (1 + len(pieces) + len(before)),
        out_specs=vmem(),
        scratch_shapes=[pltpu.VMEM((len(groups) * rows, width), BF16)],
        compiler_params=pltpu.CompilerParams(vmem_limit_bytes=VMEM_BYTES),
        cost_estimate=cost(2 * flops, 8 * count * BLK * width),
        name="early_rows",
    )(pairs, position, *pieces, *before)


def cross_kernel(components, groups, pairs_ref, position_ref, weights_ref, early_ref, *refs):
    pieces, (out_ref, left_ref, right_ref, joined_ref, done_ref, sems) = refs[:-6], refs[-6:]
    columns = weights_ref.shape[1]
    rows = pieces[0].shape[0]
    for i, piece in enumerate(pieces):
        joined_ref[i * rows : (i + 1) * rows, :] = piece[...]
    copies = []
    for q in range(out_ref.shape[0]):
        for side, rows_ref in ((0, left_ref), (1, right_ref)):
            pick = pick_group(position_ref, groups, pairs_ref[q, side])
            total = jnp.dot(pick, joined_ref[...], preferred_element_type=F32) + early_ref[2 * q + side]
            for c in range(components):
                rows_ref[q, pl.ds(c, BLK, stride=components), :] = total[:, c * columns : (c + 1) * columns]
        scaled = (left_ref[q] * weights_ref[...]).astype(BF16)
        right = right_ref[q]
        lane = lax.broadcasted_iota(jnp.int32, right.shape, 1)
        turned = pltpu.roll(right, columns // 2, 1)
        turned = jnp.where(lane < columns // 2, -turned, turned)
        for part, other in ((0, right), (1, turned)):
            other = other.astype(BF16)
            for top in range(0, scaled.shape[0], BLK):
                done_ref[q, part, top : top + BLK, :] = lax.dot_general(
                    scaled[top : top + BLK], other, (((1,), (1,)), ((), ())), preferred_element_type=F32
                ).astype(BF16)
            copy = pltpu.make_async_copy(done_ref.at[q, part], out_ref.at[q, part], sems.at[q, part])
            copy.start()
            copies.append(copy)
    for copy in copies:
        copy.wait()


def cross(pairs, position, weights, early, groups, pieces, components):
    count = pairs.shape[0]
    columns = weights.shape[1]
    rows = BLK * components
    out = jax.ShapeDtypeStruct((count, 2, rows, rows), BF16)
    return pl.pallas_call(
        functools.partial(cross_kernel, components, groups),
        out_shape=out,
        in_specs=[pl.BlockSpec(memory_space=pltpu.SMEM)] + [vmem()] * (3 + len(pieces)),
        out_specs=hbm(),
        scratch_shapes=[
            pltpu.VMEM((count, rows, columns), F32),
            pltpu.VMEM((count, rows, columns), F32),
            pltpu.VMEM((len(pieces) * pieces[0].shape[0], components * columns), BF16),
            pltpu.VMEM(out.shape, BF16),
            pltpu.SemaphoreType.DMA((count, 2)),
        ],
        compiler_params=pltpu.CompilerParams(vmem_limit_bytes=VMEM_BYTES),
        name="cross",
    )(pairs, position, weights, early, *pieces)


def shards(influence, loads, patch_order, spectral_weights, block_position, block_pairs):
    components, hot_rows, patch_cols = influence.shape
    n_patch, n_hot = lax.axis_size("patch"), lax.axis_size("hot")
    share_rows = hot_rows // n_patch
    weights = jnp.concatenate([spectral_weights, spectral_weights])[None, :]
    order = patch_order.reshape(n_patch, patch_cols // LANES, LANES)

    def swap(array, axis, k):
        size = lax.axis_size(axis)
        return lax.ppermute(array, axis, [(i, i ^ k) for i in range(size)])

    far = list(range(n_patch - 1, n_patch // 2 - 1, -1))
    near = list(range(n_patch // 2 - 1, -1, -1))
    tie = lambda value, *after: lax.optimization_barrier((value, *after))[0]

    top = n_patch // 2
    half = share_rows // 4

    def halves(i, kind):
        return [(i, 0, half, BF16), (i, half, share_rows - half, kind)]

    first_terms, my_loads = first_products(
        order, loads, influence, share_rows, far[:1], halves(0, BF16 if n_patch > 2 else F32)
    )
    rest = far[1:] + near
    cuts = []
    for i, k in enumerate(rest):
        if k >= top:
            cuts += halves(i, BF16 if k > top else F32)
        else:
            cuts.append((i, 0, share_rows, BF16 if k else F32))
    terms = list(first_terms) + list(more_products(my_loads, influence, share_rows, rest, cuts))
    straight = dict(zip(far, terms[0 : 2 * len(far) : 2]))
    lower = dict(zip(far, terms[1 : 2 * len(far) : 2]))
    carried = [swap(lower[k], "patch", k ^ top) for k in far if k != top]
    from_far = [swap(straight[k], "patch", k) for k in far]
    from_near = [
        swap(tie(term, *carried), "patch", k) for k, term in zip(near[:-1], terms[2 * len(far) :])
    ]
    passed = swap(
        summed(functools.partial(sum_kernel, BF16), tie(lower[top], *from_far[:-1]), carried, "pass_sum"), "patch", top
    )
    own = summed(
        functools.partial(total_kernel, len(from_near)), terms[-1], from_near + from_far + [passed], "share_sum"
    )

    position = block_position.reshape(n_hot * n_patch, 1, share_rows)
    patch_bits = [1 << b for b in reversed(range((n_patch - 1).bit_length()))]
    chip_bits = [2 << b for b in reversed(range((n_hot // 2 - 1).bit_length()))]

    plane = {(0, 0): own}

    def along(keys, axis, bits):
        for bit in bits:
            for j, k in list(keys):
                key = (j ^ bit, k) if axis == "hot" else (j, k ^ bit)
                plane[key] = swap(plane[j, k], axis, bit)
                keys = keys + [key]
        return keys

    def cores(keys, *after):
        mine = join([plane[key] for key in keys])
        other = swap(tie(mine, *after), "hot", 1)
        return [keys, [(j + 1, k) for j, k in keys]], [mine, other]

    def picked(group, *before):
        return early_rows(block_pairs, position, *group, before)

    along([(0, 0)], "patch", patch_bits[:1])
    near_keys = along([(0, 0)], "patch", patch_bits[1:])
    chip_keys = along([(0, 0)], "hot", chip_bits)
    head = cores([(0, 0)])
    early = picked(head)
    for key in near_keys[1:] + chip_keys[1:]:
        plane[key] = tie(plane[key], plane[0, top])
    far_keys = along([(0, top)], "patch", patch_bits[1:])
    for j, _ in chip_keys[1:]:
        start = tie(plane[j, 0], plane[0, top])
        plane[j, n_patch - 1] = swap(start, "patch", n_patch - 1)
    middle = []
    for key in near_keys[1:]:
        middle += along([key], "hot", chip_bits)[1:]
    for key in far_keys[:-1]:
        along([key], "hot", chip_bits)
    early = picked(cores(near_keys[1:] + chip_keys[1:] + [(0, top)], head[1][1]), early)
    before = early
    early = picked(cores(middle + far_keys[1:]), early)
    done = chip_keys + near_keys + [(0, top)] + middle + far_keys
    last = [key for key in plane if key not in done]
    for key in last:
        plane[key] = tie(plane[key], before)
    groups, pieces = cores(last)
    return cross(block_pairs, position, weights, early, groups, pieces, components)


def solution(mesh):
    placed = (
        P(None, "hot", "patch"),
        P("grp", None),
        P(),
        P("grp"),
        P(),
        P(("hot", "patch"), None),
    )
    return jax.shard_map(
        shards,
        mesh=mesh,
        in_specs=placed,
        out_specs=P(("grp", "hot", "patch"), None, None, None),
        check_vma=False,
    )
```
